256 devices in a mesh: blk: 128 (over z_hi, x, y, core), rep: 2 (over z_lo).
Axes of the slice: x: 4, y: 4, z: 8 (z_hi: 4, z_lo: 2; z = z_hi * 2 + z_lo), core: 2. Of those that a mesh axis runs over, the one named last changes fastest.
Arguments:
- image_hidden: bfloat16 [32768, 1152], P(('rep', 'blk')), may hold values from -6 to 6
- project_weight: bfloat16 [1152, 1152], replicated, may hold values from -0.1875 to 0.1875
- text_embed: bfloat16 [32768, 1152], P(('rep', 'blk')), may hold values from -6 to 6
- pair_ids: int32 [2, 16384], P('rep'), may hold values from 0 to 2047
- valid_count: int32 [256], P(('rep', 'blk')), may hold values from 1 to 128, as said below
- logit_scale: float32 [], replicated, may hold values from 40 to 60
- logit_bias: float32 [], replicated, may hold values from -8 to -6
Outputs:
- hidden_grad: bfloat16 [32768, 1152], P(('rep', 'blk'))
- weight_grad: float32 [1152, 1152], P('blk')
- text_grad: float32 [32768, 1152], P(('rep', 'blk'))
The draws below stay inside these ranges and needn't reach their ends.
Inputs may be any that keep to these rules, and one draw needn't show every extreme that they name: `valid_count`: pairs at positions of a block at or beyond its count are padding; in every draw some block holds 128 live pairs and some holds 1. `pair_ids`: pairs with equal labels are positives, including each pair with itself.
All inputs are finite; a program needn't handle non-finite values.
Results may differ from the reference program's by a relative error of at most 0.0064.
Values may be sent and summed in bfloat16 or wider, within the bound.
No kernel may reach another device: no remote copies, remote signals or barrier semaphores. Data moves between devices by JAX's collectives and lax.ppermute only.
A program may use at most 128 MiB of HBM per device.

```python
import jax
import jax.numpy as jnp
from jax import lax

D = 1152
B_DEV = 128
CYCLE = 16
B = 2048
GROUPS = 16
N_BLK = 128
N_REP = 2


def draw_valid_count(key, part):
    key = jax.random.fold_in(key, 7)
    first, second, third = jax.random.split(key, 3)
    total = GROUPS * CYCLE
    counts = jax.random.randint(first, (total,), 1, B_DEV + 1).astype(jnp.int32)
    highest = jax.random.randint(second, (), 0, total).astype(jnp.int32)
    lowest = (highest + 1 + jax.random.randint(third, (), 0, total - 1).astype(jnp.int32)) % total
    counts = counts.at[highest].set(B_DEV).at[lowest].set(1)
    return counts


def place_ends(entries, stream_key, smallest, top_value):
    longest = entries.shape.index(max(entries.shape))
    spots = []
    for shift in (0, 1):
        where = [jax.random.randint(jax.random.fold_in(stream_key, axis), (), 0, length) for axis, length in enumerate(entries.shape)]
        where[longest] = (where[longest] + shift) % entries.shape[longest]
        spots.append(tuple(where))
    return entries.at[spots[0]].set(smallest).at[spots[1]].set(top_value)


def block_scale(rng, dims, cuts, least, high):
    loudness, own = 1.0, jax.random.fold_in(rng, 6)
    for dim, shards_of in cuts:
        draws = jnp.exp(jax.random.uniform(jax.random.fold_in(own, dim), (shards_of,), jnp.float32, least / len(cuts), high / len(cuts)))
        loudness = loudness * jnp.repeat(draws, dims[dim] // shards_of).reshape([-1 if axis == dim else 1 for axis in range(len(dims))])
    return loudness


def normal_values(stream_key, shape, scale, most, shards=(), kind=jnp.bfloat16):
    values = jax.random.normal(stream_key, shape, jnp.float32) * scale
    if len(shards) > 0:
        values = block_scale(stream_key, shape, shards, -0.22, 0.18) * values
    return jnp.clip(values, min=-most, max=most).astype(kind)


def setup_inputs(seed: int = 0) -> dict:
    seeds = jax.random.split(jax.random.key(seed), 8)
    return {
        "image_hidden": normal_values(seeds[0], (GROUPS * B, D), 1.0, 6.0, ((0, 256),)),
        "project_weight": normal_values(seeds[1], (D, D), D ** -0.5, 0.1875),
        "text_embed": normal_values(seeds[2], (GROUPS * B, D), 1.0, 6.0, ((0, 256),)),
        "pair_ids": place_ends(jax.random.randint(seeds[3], (N_REP, N_BLK * B_DEV), 0, B), jax.random.fold_in(seeds[3], 1), 0, B - 1).astype(jnp.int32),
        "valid_count": draw_valid_count(jax.random.fold_in(seeds[7], 71), 0),
        "logit_scale": jnp.clip(jax.random.uniform(seeds[5], (), jnp.float32, 40.0, 60.0), 40.0, 60.0),
        "logit_bias": jnp.clip(jax.random.uniform(seeds[6], (), jnp.float32, -8.0, -6.0), -8.0, -6.0),
    }


epsilon = 1e-06

def one_group(hidden, project_weight, text_embed, labels, counts, logit_scale, logit_bias):
    projected = jnp.dot(hidden, project_weight, preferred_element_type=jnp.float32)
    magnitude = jnp.sqrt(lax.optimization_barrier(jnp.sum(projected * projected, axis=1, keepdims=True)) + epsilon)
    normed = projected / magnitude
    image_embed = normed.astype(jnp.bfloat16)
    text_float = text_embed.astype(jnp.float32)
    text_normed = (text_float / jnp.sqrt(lax.optimization_barrier(jnp.sum(text_float * text_float, axis=1, keepdims=True)) + epsilon)).astype(jnp.bfloat16)
    position = jnp.arange(B, dtype=jnp.int32)
    keep_row = (position % B_DEV < counts[position // B_DEV]).astype(jnp.float32)
    scores = logit_scale * jnp.dot(image_embed, text_normed.T, preferred_element_type=jnp.float32) + logit_bias
    target = jnp.where(labels[:, None] == labels[None, :], 1.0, -1.0).astype(jnp.float32)
    coefficient = (-target * jax.nn.sigmoid(-target * scores) * logit_scale * keep_row[:, None] * keep_row[None, :]).astype(jnp.bfloat16)
    embed_grad = jnp.dot(coefficient, text_normed, preferred_element_type=jnp.float32)
    text_grad = jnp.dot(coefficient.T, image_embed, preferred_element_type=jnp.float32)
    radial = lax.optimization_barrier(jnp.sum(normed * embed_grad, axis=1, keepdims=True))
    normed_grad = ((embed_grad - normed * radial) / magnitude).astype(jnp.bfloat16)
    hidden_grad = jnp.dot(normed_grad, project_weight.T, preferred_element_type=jnp.float32).astype(jnp.bfloat16)
    weight_part = jnp.dot(hidden.T, normed_grad, preferred_element_type=jnp.float32)
    return (hidden_grad, text_grad, weight_part)

def reference(image_hidden, project_weight, text_embed, pair_ids, valid_count, logit_scale, logit_bias):
    hidden_all = image_hidden.reshape(GROUPS, B, D)
    text_all = text_embed.reshape(GROUPS, B, D)
    labels_all = pair_ids.reshape(GROUPS, B)
    counts_all = valid_count.reshape(GROUPS, CYCLE)
    results = [one_group(hidden_all[group], project_weight, text_all[group], labels_all[group], counts_all[group], logit_scale, logit_bias) for group in range(GROUPS)]
    hidden_grad = jnp.concatenate([item[0] for item in results], axis=0)
    text_grad = jnp.concatenate([item[1] for item in results], axis=0)
    weight_grad = results[0][2]
    for item in results[1:]:
        weight_grad = weight_grad + item[2]
    return (hidden_grad, weight_grad, text_grad)
```

```python
import jax
import jax.numpy as jnp
import numpy as np
from jax import lax
from jax.sharding import Mesh, PartitionSpec as P

epsilon = 1e-06
AXES = ("zh", "x1", "x0", "y", "c", "zl")
SPLIT = 640
f32 = jnp.float32
bf16 = jnp.bfloat16


def dot(a, b, ca, cb):
    return lax.dot_general(a, b, (((ca,), (cb,)), ((), ())), preferred_element_type=f32)


def xor(x, axis, step):
    size = lax.axis_size(axis)
    return lax.ppermute(x, axis, [(i, i ^ step) for i in range(size)])


def row_norm(x):
    return jnp.sqrt(jnp.sum(x * x, axis=1, keepdims=True) + epsilon)


def per_device(hidden, weight, text, pair_ids, valid_count, logit_scale, logit_bias):
    rows, width = hidden.shape
    zh, y, c = (lax.axis_index(a) for a in ("zh", "y", "c"))
    x1, x0 = lax.axis_index("x1"), lax.axis_index("x0")
    x = x1 * 2 + x0
    X = ("x1", "x0")
    keep = (jnp.arange(rows) < valid_count[0])[:, None]
    with jax.named_scope("gather"):
        hid = jnp.where(keep, hidden, 0).astype(bf16)
        txt = jnp.where(keep, text, 0).astype(bf16)
        hid_x = xor(hid, "x0", 1)
        txt_2 = xor(txt, "y", 2)
        txt_1 = xor(txt, "y", 1)
        txt_3 = xor(txt, "y", 3)
        hid_2 = jnp.concatenate([hid, hid_x], 0)
        hid_c = xor(hid_2, "c", 1)
    hid_all = jnp.concatenate([hid_2, hid_c], 0)
    labels = lax.dynamic_slice_in_dim(pair_ids[0], (zh * 2 + x1) * rows * 16, rows * 16, 0)
    labels = labels.reshape(16, rows)

    def label(px, py, pc):
        return lax.dynamic_slice_in_dim(labels, (px * 4 + py) * 2 + pc, 1, 0)[0]

    hid_labels = jnp.concatenate(
        [label(x0, y, c), label(1 - x0, y, c), label(x0, y, 1 - c), label(1 - x0, y, 1 - c)]
    )
    txt_labels = jnp.concatenate([label(x0, y ^ j, c) for j in range(4)])

    def places(a, b, sa, sb, pa, pb):
        i = np.arange(576)
        r, m = i % 9, i // 9 % 4
        second, first = i // 36 % 4, i // 144
        row = ((zh ^ jnp.asarray(m)) * 288 + (pa ^ jnp.asarray(first)) * sa
               + (pb ^ jnp.asarray(second)) * sb + c * 9 + r)
        return (row[:, None] == jnp.arange(width)[None, :]).astype(bf16)

    with jax.named_scope("project"):
        projected = dot(hid_all, weight, 1, 0)
        magnitude = row_norm(projected)
        normed = projected / magnitude
        embed = normed.astype(bf16)
        hid_a = dot(places(0, 0, 72, 18, x, y), hid_all, 1, 1).astype(bf16)
        hid_b = dot(places(0, 0, 18, 72, y, x), hid_all, 1, 1).astype(bf16)
    with jax.named_scope("tile"):
        txt_all = jnp.concatenate([txt, txt_1, txt_2, txt_3], 0).astype(f32)
        txt_all = (txt_all / row_norm(txt_all)).astype(bf16)
        scores = logit_scale * dot(embed, txt_all, 1, 1) + logit_bias
        target = jnp.where(hid_labels[:, None] == txt_labels[None, :], 1.0, -1.0).astype(f32)
        coef = (-target * jax.nn.sigmoid(-target * scores) * logit_scale).astype(bf16)
        embed_grad = dot(coef, txt_all, 1, 0)
        radial = jnp.sum(normed * embed_grad, axis=1, keepdims=True)
        part = (embed_grad - normed * radial) / magnitude
        txt_part = dot(coef, embed, 0, 0)
        txt_send = txt_part.astype(bf16)
    with jax.named_scope("core"):
        arrived = xor(part.astype(bf16), "c", 1)
        half = 2 * rows
        summed = part + jnp.concatenate([arrived[half:], arrived[:half]], 0).astype(f32)
        summed_b = summed.astype(bf16)
    with jax.named_scope("weight"):
        def four(block, axis):
            got = [xor(block[k].astype(bf16), axis, k).astype(f32) for k in (2, 1, 3)]
            return block[0] + got[0] + got[1] + got[2]

        part_a = dot(hid_a, summed_b[:, :SPLIT], 1, 0).reshape(4, 144, SPLIT)
        part_b = dot(hid_b, summed_b[:, SPLIT:], 1, 0).reshape(4, 144, width - SPLIT)
        part_a = four(part_a, X)
        part_b = four(part_b, "y")
        part_a = four(part_a.reshape(4, 36, SPLIT), "y")
        part_b = four(part_b.reshape(4, 36, width - SPLIT), X)
        whole = jnp.concatenate([part_a, part_b], 1)
        whole = whole + xor(whole.astype(bf16), "zl", 1).astype(f32)
        weight_grad = four(whole.reshape(4, 9, width), "zh")
    with jax.named_scope("hidden"):
        own = summed[:rows] + xor(summed_b[rows:half], "x0", 1).astype(f32)
        hidden_grad = dot(own.astype(bf16), weight, 1, 1)
        hidden_grad = jnp.where(keep, hidden_grad, 0.0).astype(bf16)
    with jax.named_scope("text"):
        got = [xor(txt_send[j * rows : (j + 1) * rows], "y", j).astype(f32) for j in (2, 1, 3)]
        text_grad = jnp.where(keep, txt_part[:rows] + got[0] + got[1] + got[2], 0.0)
    return hidden_grad, weight_grad, text_grad


def solution(mesh):
    fine = Mesh(mesh.devices.reshape(4, 2, 2, 4, 2, 2), AXES)
    blk = ("zh", "x1", "x0", "y", "c")
    by_row = P(("zl",) + blk, None)
    return jax.shard_map(
        per_device,
        mesh=fine,
        in_specs=(by_row, P(), by_row, P("zl", None), P(("zl",) + blk), P(), P()),
        out_specs=(by_row, P(blk, None), by_row),
        check_vma=False,
    )
```

```python
import jax
import jax.numpy as jnp
import numpy as np
from jax import lax
from jax.experimental import pallas as pl
from jax.experimental.pallas import tpu as pltpu
from jax.sharding import Mesh, PartitionSpec as P

epsilon = 1e-06
AXES = ("zh", "x1", "x0", "y", "c", "zl")
f32 = jnp.float32
bf16 = jnp.bfloat16
ROWS = 128
WIDTH = 1152
VMEM = pl.BlockSpec(memory_space=pltpu.VMEM)
SMEM = pl.BlockSpec(memory_space=pltpu.SMEM)


def dot(a, b, ca, cb):
    return lax.dot_general(a, b, (((ca,), (cb,)), ((), ())), preferred_element_type=f32)


def xor(x, axis, step):
    size = lax.axis_size(axis)
    return lax.ppermute(x, axis, [(i, i ^ step) for i in range(size)])


def shape(dtype, *dims):
    return jax.ShapeDtypeStruct(dims, dtype)


def call(body, outs, specs, flops, moved, scratch=()):
    return pl.pallas_call(
        body,
        out_shape=outs,
        in_specs=specs,
        out_specs=[VMEM] * len(outs),
        scratch_shapes=scratch,
        compiler_params=pltpu.CompilerParams(vmem_limit_bytes=40 << 20),
        cost_estimate=pl.CostEstimate(flops=flops, bytes_accessed=moved, transcendentals=0),
    )


def prepare(count, hidden, text, hid_out, txt_out):
    keep = lax.broadcasted_iota(jnp.int32, (ROWS, 1), 0) < count[0]
    hid_out[...] = jnp.where(keep, hidden[...].astype(f32), 0.0).astype(bf16)
    txt = text[...].astype(f32)
    txt = txt * lax.rsqrt(jnp.sum(txt * txt, axis=1, keepdims=True) + epsilon)
    txt_out[...] = jnp.where(keep, txt, 0.0).astype(bf16)


def project(own, paired, cores, weight, places, embed, normed, inverse, turned):
    hid = jnp.concatenate([own[...], paired[...], cores[...]], 0)
    projected = dot(hid, weight[...], 1, 0)
    inv = lax.rsqrt(jnp.sum(projected * projected, axis=1, keepdims=True) + epsilon)
    unit = projected * inv
    normed[...] = unit
    embed[...] = unit.astype(bf16)
    inverse[...] = inv
    spots = lax.broadcasted_iota(jnp.int32, (576, WIDTH), 1)
    chosen = (spots == places[...]).astype(f32).astype(bf16)
    turned[...] = dot(chosen, hid, 1, 1).astype(bf16)


def tile(where, scalars, labels, embed, normed, inverse, t0, t1, t2, t3, coef_out, part_out, part_send):
    txt = jnp.concatenate([t0[...], t1[...], t2[...], t3[...]], 0)
    left = [
        jnp.transpose(jnp.broadcast_to(labels[pl.ds(where[k], 1), :], (8, ROWS)))[:, :1]
        for k in range(4)
    ]
    right = [labels[pl.ds(where[4 + k], 1), :] for k in range(4)]
    left = jnp.concatenate(left, 0)
    right = jnp.concatenate(right, 1)
    scores = scalars[0] * dot(embed[...], txt, 1, 1) + scalars[1]
    target = jnp.where(left == right, 1.0, -1.0).astype(f32)
    coef = (-target * jax.nn.sigmoid(-target * scores) * scalars[0]).astype(bf16)
    coef_out[...] = coef
    grad = dot(coef, txt, 1, 0)
    unit = normed[...]
    radial = jnp.sum(unit * grad, axis=1, keepdims=True)
    part = (grad - unit * radial) * inverse[...]
    part_out[...] = part
    part_send[...] = part.astype(bf16)


def text_terms(coef, embed, own, s1, s2, s3):
    terms = dot(coef[...], embed[...], 0, 0)
    own[...] = terms[:ROWS]
    for k, out in enumerate((s1, s2, s3)):
        out[...] = terms[(k + 1) * ROWS : (k + 2) * ROWS].astype(bf16)


def weight_terms(part, arrived, turned, own_rows, send_rows, own, s1, s2, s3):
    half = 2 * ROWS
    top = part[:half] + arrived[half:].astype(f32)
    low = part[half:] + arrived[:half].astype(f32)
    own_rows[...] = top[:ROWS]
    send_rows[...] = top[ROWS:].astype(bf16)
    summed = jnp.concatenate([top, low], 0).astype(bf16)
    terms = dot(turned[...], summed, 1, 0)
    own[...] = terms[:144]
    for k, out in enumerate((s1, s2, s3)):
        out[...] = terms[(k + 1) * 144 : (k + 2) * 144].astype(bf16)


def back(count, own, arrived, weight, out):
    rows = (own[...] + arrived[...].astype(f32)).astype(bf16)
    grad = dot(rows, weight[...], 1, 1)
    keep = lax.broadcasted_iota(jnp.int32, (ROWS, 1), 0) < count[0]
    out[...] = jnp.where(keep, grad, 0.0).astype(bf16)


def four(own, sends, axis):
    got = [xor(sends[k - 1], axis, k).astype(f32) for k in (2, 1, 3)]
    return own + got[0] + got[1] + got[2]


def per_device(hidden, weight, text, pair_ids, valid_count, logit_scale, logit_bias):
    zh, x1, x0, y, c = (lax.axis_index(a) for a in ("zh", "x1", "x0", "y", "c"))
    x = x1 * 2 + x0
    X = ("x1", "x0")
    block = ROWS * WIDTH
    labels = lax.dynamic_slice_in_dim(pair_ids[0], (zh * 2 + x1) * ROWS * 16, ROWS * 16, 0)
    labels = labels.reshape(16, ROWS)
    where = [(px * 4 + y) * 2 + pc for pc, px in ((c, x0), (c, 1 - x0), (1 - c, x0), (1 - c, 1 - x0))]
    where = jnp.stack(where + [(x0 * 4 + (y ^ j)) * 2 + c for j in range(4)]).astype(jnp.int32)
    scalars = jnp.stack([logit_scale, logit_bias])
    i = np.arange(576)
    places = (
        ((zh ^ jnp.asarray(i // 9 % 4)) * 288)
        + ((x ^ jnp.asarray(i // 144)) * 72)
        + ((y ^ jnp.asarray(i // 36 % 4)) * 18)
        + (c * 9 + jnp.asarray(i % 9))
    ).astype(jnp.int32)[:, None]
    with jax.named_scope("prepare"):
        hid, txt = call(
            prepare, [shape(bf16, ROWS, WIDTH)] * 2, [SMEM, VMEM, VMEM], block * 8, block * 8
        )(valid_count, hidden, text)
    with jax.named_scope("gather"):
        hid_x = xor(hid, "x0", 1)
        txt_2 = xor(txt, "y", 2)
        txt_1 = xor(txt, "y", 1)
        txt_3 = xor(txt, "y", 3)
        hid_c = xor(jnp.concatenate([hid, hid_x], 0), "c", 1)
    with jax.named_scope("project"):
        embed, normed, inverse, turned = call(
            project,
            [shape(bf16, 512, WIDTH), shape(f32, 512, WIDTH), shape(f32, 512, 1), shape(bf16, 576, 512)],
            [VMEM] * 5,
            2 * 512 * WIDTH * 1728,
            WIDTH * (WIDTH * 2 + 512 * 8),
        )(hid, hid_x, hid_c, weight, places)
    with jax.named_scope("tile"):
        coef, part, part_send = call(
            tile,
            [shape(bf16, 512, 512), shape(f32, 512, WIDTH), shape(bf16, 512, WIDTH)],
            [SMEM, SMEM] + [VMEM] * 8,
            4 * 512 * 512 * WIDTH,
            WIDTH * 512 * 14,
        )(where, scalars, labels, embed, normed, inverse, txt, txt_1, txt_2, txt_3)
    with jax.named_scope("core"):
        arrived = xor(part_send, "c", 1)
    with jax.named_scope("text"):
        txt_own, *txt_sends = call(
            text_terms,
            [shape(f32, ROWS, WIDTH)] + [shape(bf16, ROWS, WIDTH)] * 3,
            [VMEM] * 2,
            2 * 512 * 512 * WIDTH,
            WIDTH * 512 * 5,
        )(coef, embed)
    with jax.named_scope("weight"):
        own_rows, send_rows, own, *sends = call(
            weight_terms,
            [shape(f32, ROWS, WIDTH), shape(bf16, ROWS, WIDTH), shape(f32, 144, WIDTH)]
            + [shape(bf16, 144, WIDTH)] * 3,
            [VMEM] * 3,
            2 * 512 * 576 * WIDTH,
            WIDTH * 512 * 10,
        )(part, arrived, turned)
        whole = four(own, sends, X).reshape(4, 36, WIDTH)
        whole = four(whole[0], [whole[k].astype(bf16) for k in (1, 2, 3)], "y")
        whole = whole + xor(whole.astype(bf16), "zl", 1).astype(f32)
        whole = whole.reshape(4, 9, WIDTH)
        weight_grad = four(whole[0], [whole[k] for k in (1, 2, 3)], "zh")
    with jax.named_scope("hidden"):
        rows_x = xor(send_rows, "x0", 1)
        (hidden_grad,) = call(
            back,
            [shape(bf16, ROWS, WIDTH)],
            [SMEM] + [VMEM] * 3,
            2 * block * WIDTH,
            WIDTH * WIDTH * 2 + block * 8,
        )(valid_count, own_rows, rows_x, weight)
    with jax.named_scope("text"):
        keep = (jnp.arange(ROWS) < valid_count[0])[:, None]
        text_grad = jnp.where(keep, four(txt_own, txt_sends, "y"), 0.0)
    return hidden_grad, weight_grad, text_grad


def solution(mesh):
    fine = Mesh(mesh.devices.reshape(4, 2, 2, 4, 2, 2), AXES)
    blk = ("zh", "x1", "x0", "y", "c")
    by_row = P(("zl",) + blk, None)
    return jax.shard_map(
        per_device,
        mesh=fine,
        in_specs=(by_row, P(), by_row, P("zl", None), P(("zl",) + blk), P(), P()),
        out_specs=(by_row, P(blk, None), by_row),
        check_vma=False,
    )
```

```python
import jax
import jax.numpy as jnp
import numpy as np
from jax import lax
from jax.experimental import pallas as pl
from jax.experimental.pallas import tpu as pltpu
from jax.sharding import Mesh, PartitionSpec as P

epsilon = 1e-06
AXES = ("zh", "x1", "x0", "y", "c", "zl")
f32 = jnp.float32
bf16 = jnp.bfloat16
ROWS = 128
WIDTH = 1152
VMEM = pl.BlockSpec(memory_space=pltpu.VMEM)
SMEM = pl.BlockSpec(memory_space=pltpu.SMEM)
HBM = pl.BlockSpec(memory_space=pltpu.HBM)


def dot(a, b, ca, cb):
    return lax.dot_general(a, b, (((ca,), (cb,)), ((), ())), preferred_element_type=f32)


def xor(x, axis, step):
    size = lax.axis_size(axis)
    return lax.ppermute(x, axis, [(i, i ^ step) for i in range(size)])


def shape(dtype, *dims):
    return jax.ShapeDtypeStruct(dims, dtype)


def in_hbm(x):
    return pltpu.with_memory_space_constraint(x, pltpu.HBM)


def call(body, outs, specs, flops, moved, scratch=()):
    return pl.pallas_call(
        body,
        out_shape=outs,
        in_specs=specs,
        out_specs=[VMEM] * len(outs),
        scratch_shapes=scratch,
        compiler_params=pltpu.CompilerParams(vmem_limit_bytes=40 << 20),
        cost_estimate=pl.CostEstimate(flops=flops, bytes_accessed=moved, transcendentals=0),
    )


def prepare(count, hidden, text, hid_out, txt_out, hid_in, txt_in, sems):
    copies = [
        pltpu.make_async_copy(text, txt_in, sems.at[0]),
        pltpu.make_async_copy(hidden, hid_in, sems.at[1]),
    ]
    for copy in copies:
        copy.start()
    keep = lax.broadcasted_iota(jnp.int32, (ROWS, 1), 0) < count[0]
    copies[0].wait()
    txt = txt_in[...].astype(f32)
    txt = txt * lax.rsqrt(jnp.sum(txt * txt, axis=1, keepdims=True) + epsilon)
    txt_out[...] = jnp.where(keep, txt, 0.0).astype(bf16)
    copies[1].wait()
    hid_out[...] = jnp.where(keep, hid_in[...].astype(f32), 0.0).astype(bf16)


def join(own, paired, t1, t3, both, first, second):
    both[:ROWS] = own[...]
    both[ROWS:] = paired[...]
    first[...] = t3[: ROWS // 2]
    second[...] = t1[ROWS // 2 :]


def project(both, cores, weight, places, embed, normed, inverse, turned, held, sem):
    copy = pltpu.make_async_copy(weight, held, sem)
    copy.start()
    hid = jnp.concatenate([both[...], cores[...]], 0)
    spots = lax.broadcasted_iota(jnp.int32, (576, WIDTH), 1)
    chosen = (spots == places[...]).astype(f32).astype(bf16)
    turned[...] = dot(chosen, hid, 1, 1).astype(bf16)
    copy.wait()
    projected = dot(hid, held[...], 1, 0)
    inv = lax.rsqrt(jnp.sum(projected * projected, axis=1, keepdims=True) + epsilon)
    unit = projected * inv
    normed[...] = unit
    embed[...] = unit.astype(bf16)
    inverse[...] = inv


def tile(where, scalars, labels, embed, normed, inverse, t0, t1, t2a, t2b, t3, coef_out, part_out, part_send):
    txt = jnp.concatenate([t0[...], t1[...], t2a[...], t2b[...], t3[...]], 0)
    left = [
        jnp.transpose(jnp.broadcast_to(labels[pl.ds(where[k], 1), :], (8, ROWS)))[:, :1]
        for k in range(4)
    ]
    right = [labels[pl.ds(where[4 + k], 1), :] for k in range(4)]
    left = jnp.concatenate(left, 0)
    right = jnp.concatenate(right, 1)
    scores = scalars[0] * dot(embed[...], txt, 1, 1) + scalars[1]
    target = jnp.where(left == right, 1.0, -1.0).astype(f32)
    coef = (-target * jax.nn.sigmoid(-target * scores) * scalars[0]).astype(bf16)
    coef_out[...] = coef
    grad = dot(coef, txt, 1, 0)
    unit = normed[...]
    radial = jnp.sum(unit * grad, axis=1, keepdims=True)
    part = (grad - unit * radial) * inverse[...]
    part_out[...] = part
    part_send[...] = part.astype(bf16)


def text_terms(coef, embed, terms):
    terms[...] = dot(coef[...], embed[...], 0, 0)


def weight_terms(part, arrived, turned, terms, rows, own, s1, s2, s3, t1, t2):
    half = 2 * ROWS
    top = part[:half] + arrived[half:].astype(f32)
    low = part[half:] + arrived[:half].astype(f32)
    rows[...] = top
    summed = jnp.concatenate([top, low], 0).astype(bf16)
    grad = dot(turned[...], summed, 1, 0)
    own[...] = grad[:144]
    for k, out in enumerate((s1, s2, s3)):
        out[...] = grad[(k + 1) * 144 : (k + 2) * 144].astype(bf16)
    for k, out in enumerate((t1, t2)):
        out[...] = terms[(k + 1) * ROWS : (k + 2) * ROWS].astype(bf16)


def first_sum(own, a1, a2, a3, terms, b1, b2, rows, out, text, text_send, send):
    out[...] = own[...] + a2[...].astype(f32) + a1[...].astype(f32) + a3[...].astype(f32)
    text[...] = terms[:ROWS] + b2[...].astype(f32) + b1[...].astype(f32)
    text_send[...] = terms[3 * ROWS :].astype(bf16)
    send[...] = rows[ROWS:].astype(bf16)


def second_sum(own, a1, a2, a3, out, send):
    total = own[...] + a2[...].astype(f32) + a1[...].astype(f32) + a3[...].astype(f32)
    out[...] = total
    send[...] = total.astype(bf16)


def third_sum(count, own, a1, text, b3, rows, arrived, out, text_grad, grad):
    out[...] = own[...] + a1[...].astype(f32)
    keep = lax.broadcasted_iota(jnp.int32, (ROWS, 1), 0) < count[0]
    text_grad[...] = jnp.where(keep, text[...] + b3[...].astype(f32), 0.0)
    grad[...] = (rows[:ROWS] + arrived[...].astype(f32)).astype(bf16)


def back(count, rows, weight, out):
    grad = dot(rows[...], weight[...], 1, 1)
    keep = lax.broadcasted_iota(jnp.int32, (ROWS, 1), 0) < count[0]
    out[...] = jnp.where(keep, grad, 0.0).astype(bf16)


def four(own, sends, axis):
    got = [xor(sends[k - 1], axis, k).astype(f32) for k in (2, 1, 3)]
    return own + got[0] + got[1] + got[2]


def per_device(hidden, weight, text, pair_ids, valid_count, logit_scale, logit_bias):
    zh, x1, x0, y, c = (lax.axis_index(a) for a in ("zh", "x1", "x0", "y", "c"))
    x = x1 * 2 + x0
    X = ("x1", "x0")
    block = ROWS * WIDTH
    labels = lax.dynamic_slice_in_dim(pair_ids[0], (zh * 2 + x1) * ROWS * 16, ROWS * 16, 0)
    labels = labels.reshape(16, ROWS)
    where = [(px * 4 + y) * 2 + pc for pc, px in ((c, x0), (c, 1 - x0), (1 - c, x0), (1 - c, 1 - x0))]
    where = jnp.stack(where + [(x0 * 4 + (y ^ j)) * 2 + c for j in range(4)]).astype(jnp.int32)
    scalars = jnp.stack([logit_scale, logit_bias])
    i = np.arange(576)
    places = (
        ((zh ^ jnp.asarray(i // 9 % 4)) * 288)
        + ((x ^ jnp.asarray(i // 144)) * 72)
        + ((y ^ jnp.asarray(i // 36 % 4)) * 18)
        + (c * 9 + jnp.asarray(i % 9))
    ).astype(jnp.int32)[:, None]
    wide, tall = shape(bf16, ROWS, WIDTH), shape(f32, 512, WIDTH)
    with jax.named_scope("prepare"):
        hid, txt = call(
            prepare,
            [wide, wide],
            [SMEM, HBM, HBM],
            0,
            block,
            [pltpu.VMEM((ROWS, WIDTH), bf16)] * 2 + [pltpu.SemaphoreType.DMA((2,))],
        )(valid_count, in_hbm(hidden), in_hbm(text))
    with jax.named_scope("gather"):
        hid_x = xor(hid, "x0", 1)
        txt_1 = xor(txt, "y", 1)
        txt_3 = xor(txt, "y", 3)
        both, first, second = call(
            join,
            [shape(bf16, 256, WIDTH)] + [shape(bf16, 64, WIDTH)] * 2,
            [VMEM] * 4,
            0,
            block,
        )(hid, hid_x, txt_1, txt_3)
        txt_2a = xor(first, "y", 1)
        txt_2b = xor(second, "y", 3)
        hid_c = xor(both, "c", 1)
    with jax.named_scope("project"):
        embed, normed, inverse, turned = call(
            project,
            [shape(bf16, 512, WIDTH), tall, shape(f32, 512, 1), shape(bf16, 576, 512)],
            [VMEM, VMEM, HBM, VMEM],
            0,
            block,
            [pltpu.VMEM((WIDTH, WIDTH), bf16), pltpu.SemaphoreType.DMA],
        )(both, hid_c, in_hbm(weight), places)
    with jax.named_scope("tile"):
        coef, part, part_send = call(
            tile,
            [shape(bf16, 512, 512), tall, shape(bf16, 512, WIDTH)],
            [SMEM, SMEM] + [VMEM] * 9,
            0,
            block,
        )(where, scalars, labels, embed, normed, inverse, txt, txt_1, txt_2a, txt_2b, txt_3)
    with jax.named_scope("core"):
        arrived = xor(part_send, "c", 1)
    with jax.named_scope("text"):
        (terms,) = call(text_terms, [tall], [VMEM] * 2, 0, block)(coef, embed)
    with jax.named_scope("weight"):
        rows, own, s1, s2, s3, u1, u2 = call(
            weight_terms,
            [shape(f32, 256, WIDTH), shape(f32, 144, WIDTH)]
            + [shape(bf16, 144, WIDTH)] * 3
            + [wide] * 2,
            [VMEM] * 4,
            0,
            block,
        )(part, arrived, turned, terms)
        s2, s1, s3 = xor(s2, X, 2), xor(s1, X, 1), xor(s3, X, 3)
        u2, u1 = xor(u2, "y", 2), xor(u1, "y", 1)
        whole, text_sum, u3, rows_send = call(
            first_sum,
            [shape(f32, 144, WIDTH), shape(f32, ROWS, WIDTH), wide, wide],
            [VMEM] * 8,
            0,
            block,
        )(own, s1, s2, s3, terms, u1, u2, rows)
        whole = whole.reshape(4, 36, WIDTH)
        s2, s1, s3 = (xor(whole[k].astype(bf16), "y", k) for k in (2, 1, 3))
        rows_x = xor(rows_send, "x0", 1)
        u3 = xor(u3, "y", 3)
        small = shape(f32, 36, WIDTH)
        whole, whole_send = call(
            second_sum, [small, shape(bf16, 36, WIDTH)], [VMEM] * 4, 0, block
        )(whole[0], s1, s2, s3)
        whole, text_grad, grad = call(
            third_sum,
            [small, shape(f32, ROWS, WIDTH), wide],
            [SMEM] + [VMEM] * 6,
            0,
            block,
        )(valid_count, whole, xor(whole_send, "zl", 1), text_sum, u3, rows, rows_x)
        whole = whole.reshape(4, 9, WIDTH)
        weight_grad = four(whole[0], [whole[k] for k in (1, 2, 3)], "zh")
    with jax.named_scope("hidden"):
        (hidden_grad,) = call(
            back, [wide], [SMEM] + [VMEM] * 2, 2 * block * WIDTH, WIDTH * WIDTH * 2
        )(valid_count, grad, weight)
    return hidden_grad, weight_grad, text_grad


def solution(mesh):
    fine = Mesh(mesh.devices.reshape(4, 2, 2, 4, 2, 2), AXES)
    blk = ("zh", "x1", "x0", "y", "c")
    by_row = P(("zl",) + blk, None)
    return jax.shard_map(
        per_device,
        mesh=fine,
        in_specs=(by_row, P(), by_row, P("zl", None), P(("zl",) + blk), P(), P()),
        out_specs=(by_row, P(blk, None), by_row),
        check_vma=False,
    )
```

```python
import jax
import jax.numpy as jnp
from jax import lax
from jax.experimental import pallas as pl
from jax.experimental.pallas import tpu as pltpu
from jax.sharding import Mesh, PartitionSpec as P

epsilon = 1e-06
AXES = ("zh", "x1", "x0", "y", "c", "zl")
f32 = jnp.float32
bf16 = jnp.bfloat16
ROWS = 128
WIDTH = 1152
VMEM = pl.BlockSpec(memory_space=pltpu.VMEM)
SMEM = pl.BlockSpec(memory_space=pltpu.SMEM)
ANY = pl.BlockSpec(memory_space=pl.ANY)
HBM = pl.BlockSpec(memory_space=pltpu.HBM)


def dot(a, b, ca, cb):
    return lax.dot_general(a, b, (((ca,), (cb,)), ((), ())), preferred_element_type=f32)


def xor(x, axis, step):
    size = lax.axis_size(axis)
    return lax.ppermute(x, axis, [(i, i ^ step) for i in range(size)])


def shape(dtype, *dims):
    return jax.ShapeDtypeStruct(dims, dtype)


def in_hbm(x):
    return pltpu.with_memory_space_constraint(x, pltpu.HBM)


def call(body, outs, specs, flops, moved, scratch=()):
    return pl.pallas_call(
        body,
        out_shape=outs,
        in_specs=specs,
        out_specs=[VMEM] * len(outs),
        scratch_shapes=scratch,
        compiler_params=pltpu.CompilerParams(vmem_limit_bytes=40 << 20),
        cost_estimate=pl.CostEstimate(flops=flops, bytes_accessed=moved, transcendentals=0),
    )


def prepare(count, hidden, text, hid_out, txt_out, hid_in, txt_in, sems):
    copies = [
        pltpu.make_async_copy(text, txt_in, sems.at[0]),
        pltpu.make_async_copy(hidden, hid_in, sems.at[1]),
    ]
    for copy in copies:
        copy.start()
    keep = lax.broadcasted_iota(jnp.int32, (ROWS, 1), 0) < count[0]
    copies[0].wait()
    txt = txt_in[...].astype(f32)
    txt = txt * lax.rsqrt(jnp.sum(txt * txt, axis=1, keepdims=True) + epsilon)
    txt_out[...] = jnp.where(keep, txt, 0.0).astype(bf16)
    copies[1].wait()
    hid_out[...] = jnp.where(keep, hid_in[...].astype(f32), 0.0).astype(bf16)


def join(after, own, paired, t1, t3, both, first, second):
    both[:ROWS] = own[...]
    both[ROWS:] = paired[...]
    first[...] = t3[: ROWS // 2]
    second[...] = t1[ROWS // 2 :]


def ahead(after, pair_ids, weight, held, chosen, left, right, sem):
    copy = pltpu.make_async_copy(weight, held, sem)
    copy.start()
    zh, x1, x0, y, c, zl = (lax.axis_index(a) for a in AXES)
    row = lax.broadcasted_iota(jnp.int32, (576, 1), 0)
    k, row = row // 144, row % 144
    j, row = row // 36, row % 36
    m, r = row // 9, row % 9
    turn = jnp.where(zl == 0, 4 - m, m)
    owner = (zh + turn) % 4
    place = owner * 288 + (k ^ (x1 * 2 + x0)) * 72 + (j ^ y) * 18 + c * 9 + r
    spots = lax.broadcasted_iota(jnp.int32, (576, WIDTH), 1)
    chosen[...] = (spots == place).astype(f32).astype(bf16)
    base = (zh * 2 + x1) * 16

    def label(px, py, pc):
        start = pl.multiple_of((base + (px * 4 + py) * 2 + pc) * ROWS, ROWS)
        return pair_ids[:, pl.ds(start, ROWS)]

    for k, (px, pc) in enumerate(((x0, c), (1 - x0, c), (x0, 1 - c), (1 - x0, 1 - c))):
        tall = jnp.transpose(jnp.broadcast_to(label(px, y, pc), (8, ROWS)))
        left[k * ROWS : (k + 1) * ROWS, :] = tall[:, :1]
    for j in range(4):
        right[:, j * ROWS : (j + 1) * ROWS] = label(x0, y ^ j, c)
    copy.wait()


def project(hid, weight, chosen, embed, normed, inverse, turned):
    projected = dot(hid[...], weight[...], 1, 0)
    turned[...] = dot(chosen[...], hid[...], 1, 1).astype(bf16)
    inv = lax.rsqrt(jnp.sum(projected * projected, axis=1, keepdims=True) + epsilon)
    unit = projected * inv
    normed[...] = unit
    embed[...] = unit.astype(bf16)
    inverse[...] = inv


def tile(scale, bias, left, right, e0, e1, n0, n1, i0, i1, t0, t1, t2a, t2b, t3, coef_out, part_out, part_send):
    txt = jnp.concatenate([t0[...], t1[...], t2a[...], t2b[...], t3[...]], 0)
    embed = jnp.concatenate([e0[...], e1[...]], 0)
    scores = scale[0] * dot(embed, txt, 1, 1) + bias[0]
    target = jnp.where(left[...] == right[...], 1.0, -1.0).astype(f32)
    coef = (-target * jax.nn.sigmoid(-target * scores) * scale[0]).astype(bf16)
    coef_out[...] = coef
    grad = dot(coef, txt, 1, 0)
    for k, (unit, inverse) in enumerate(((n0, i0), (n1, i1))):
        half = slice(k * 256, (k + 1) * 256)
        radial = jnp.sum(unit[...] * grad[half], axis=1, keepdims=True)
        part = (grad[half] - unit[...] * radial) * inverse[...]
        part_out[half, :] = part
        part_send[half, :] = part.astype(bf16)


def text_terms(coef, e0, e1, terms):
    terms[...] = dot(coef[:256], e0[...], 0, 0) + dot(coef[256:], e1[...], 0, 0)


def weight_terms(part, arrived, h0, h1, terms, rows, own, s1, s2, s3, t1, t2, t3):
    half = 2 * ROWS
    top = part[:half] + arrived[half:].astype(f32)
    low = part[half:] + arrived[:half].astype(f32)
    rows[...] = top
    grad = dot(h0[...], top.astype(bf16), 1, 0) + dot(h1[...], low.astype(bf16), 1, 0)
    own[...] = grad[:144]
    for k, out in enumerate((s1, s2, s3)):
        out[...] = grad[(k + 1) * 144 : (k + 2) * 144].astype(bf16)
    for k, out in enumerate((t1, t2, t3)):
        out[...] = terms[(k + 1) * ROWS : (k + 2) * ROWS].astype(bf16)


def first_sum(own, a1, a2, a3, b1, b2, b3, out, s1, s2, s3, held):
    held[...] = own[...] + a2[...].astype(f32) + a1[...].astype(f32) + a3[...].astype(f32)
    out[...] = held[:36]
    for k, send in enumerate((s1, s2, s3)):
        send[...] = held[(k + 1) * 36 : (k + 2) * 36].astype(bf16)


def second_sum(own, a1, a2, a3, rows, send, rows_send):
    total = own[...] + a2[...].astype(f32) + a1[...].astype(f32) + a3[...].astype(f32)
    send[...] = total.astype(bf16)
    rows_send[...] = rows[ROWS:].astype(bf16)


def third_sum(own, arrived, out, near, far, mine, held):
    mine[...] = own[...].astype(f32)
    held[...] = arrived[...].astype(f32)
    out[...] = mine[:9] + held[:9]
    near[...] = mine[9:18] + held[27:36]
    far[...] = mine[18:27] + held[18:27]


def last_sum(after, own, a1, a2, a3, out):
    out[...] = own[...] + (a1[...] + a2[...]) + a3[...]


def text_sum(after, count, terms, b1, b2, b3, out):
    keep = lax.broadcasted_iota(jnp.int32, (ROWS, 1), 0) < count[0]
    total = terms[:ROWS] + b2[...].astype(f32) + b1[...].astype(f32) + b3[...].astype(f32)
    out[...] = jnp.where(keep, total, 0.0)


def back(count, rows, arrived, weight, out, done):
    total = (rows[:ROWS] + arrived[...].astype(f32)).astype(bf16)
    grad = dot(total, weight[...], 1, 1)
    keep = lax.broadcasted_iota(jnp.int32, (ROWS, 1), 0) < count[0]
    out[...] = jnp.where(keep, grad, 0.0).astype(bf16)
    done[...] = jnp.zeros((8, ROWS), f32)


def per_device(hidden, weight, text, pair_ids, valid_count, logit_scale, logit_bias):
    X = ("x1", "x0")
    block = ROWS * WIDTH
    wide, tall = shape(bf16, ROWS, WIDTH), shape(f32, 512, WIDTH)
    with jax.named_scope("prepare"):
        hid, txt = call(
            prepare,
            [wide, wide],
            [SMEM, HBM, HBM],
            0,
            block,
            [pltpu.VMEM((ROWS, WIDTH), bf16)] * 2 + [pltpu.SemaphoreType.DMA((2,))],
        )(valid_count, in_hbm(hidden), in_hbm(text))
    with jax.named_scope("gather"):
        hid_x = xor(hid, "x0", 1)
        txt_1 = xor(txt, "y", 1)
        txt_3 = xor(txt, "y", 3)
        held, chosen, left, right = call(
            ahead,
            [
                shape(bf16, WIDTH, WIDTH),
                shape(bf16, 576, WIDTH),
                shape(jnp.int32, 512, 1),
                shape(jnp.int32, 1, 512),
            ],
            [ANY, VMEM, HBM],
            block * 1000,
            block,
            [pltpu.SemaphoreType.DMA],
        )(hid, pair_ids, in_hbm(weight))
        both, first, second = call(
            join,
            [shape(bf16, 256, WIDTH)] + [shape(bf16, 64, WIDTH)] * 2,
            [ANY] + [VMEM] * 4,
            0,
            block,
        )(chosen, hid, hid_x, txt_1, txt_3)
        txt_2a = xor(first, "y", 1)
        txt_2b = xor(second, "y", 3)
        hid_c = xor(both, "c", 1)
    with jax.named_scope("project"):
        outs = [shape(bf16, 256, WIDTH), shape(f32, 256, WIDTH), shape(f32, 256, 1), shape(bf16, 576, 256)]
        run = call(project, outs, [VMEM] * 3, 0, block)
        e0, n0, i0, h0 = run(both, held, chosen)
        e1, n1, i1, h1 = run(hid_c, held, chosen)
    with jax.named_scope("tile"):
        coef, part, part_send = call(
            tile,
            [shape(bf16, 512, 512), tall, shape(bf16, 512, WIDTH)],
            [SMEM, SMEM] + [VMEM] * 13,
            0,
            block,
        )(
            logit_scale.reshape(1), logit_bias.reshape(1), left, right,
            e0, e1, n0, n1, i0, i1, txt, txt_1, txt_2a, txt_2b, txt_3,
        )
    with jax.named_scope("core"):
        arrived = xor(part_send, "c", 1)
    with jax.named_scope("text"):
        (terms,) = call(text_terms, [tall], [VMEM] * 3, 0, block)(coef, e0, e1)
    with jax.named_scope("weight"):
        rows, own, s1, s2, s3, u1, u2, u3 = call(
            weight_terms,
            [shape(f32, 256, WIDTH), shape(f32, 144, WIDTH)]
            + [shape(bf16, 144, WIDTH)] * 3
            + [wide] * 3,
            [VMEM] * 5,
            0,
            block,
        )(part, arrived, h0, h1, terms)
        s2, s1, s3 = xor(s2, X, 2), xor(s1, X, 1), xor(s3, X, 3)
        u1, u3, u2 = xor(u1, "y", 1), xor(u3, "y", 3), xor(u2, "y", 2)
        small, small_b = shape(f32, 36, WIDTH), shape(bf16, 36, WIDTH)
        whole, s1, s2, s3 = call(
            first_sum,
            [small] + [small_b] * 3,
            [VMEM] * 4 + [ANY] * 3,
            0,
            block,
            [pltpu.VMEM((144, WIDTH), f32)],
        )(own, s1, s2, s3, u1, u2, u3)
        s2, s1, s3 = xor(s2, "y", 2), xor(s1, "y", 1), xor(s3, "y", 3)
        whole_send, rows_send = call(second_sum, [small_b, wide], [VMEM] * 5, 0, block)(
            whole, s1, s2, s3, rows
        )
        arrived = xor(whole_send, "zl", 1)
        whole, near, far = call(
            third_sum,
            [shape(f32, 9, WIDTH)] * 3,
            [VMEM] * 2,
            0,
            block,
            [pltpu.VMEM((36, WIDTH), f32)] * 2,
        )(whole_send, arrived)
        Z = ("zh", "zl")
        steps = (near, 1), (near, 2), (far, 3)
        got = [
            lax.ppermute(x, Z, [(p, (p + (hop if p % 2 else -hop)) % 8) for p in range(8)])
            for x, hop in steps
        ]
    with jax.named_scope("hidden"):
        rows_x = xor(rows_send, "x0", 1)
        hidden_grad, done = call(
            back, [wide, shape(f32, 8, ROWS)], [SMEM] + [VMEM] * 3, 2 * block * WIDTH, WIDTH * WIDTH * 2
        )(valid_count, rows, rows_x, held)
    with jax.named_scope("weight"):
        (weight_grad,) = call(last_sum, [shape(f32, 9, WIDTH)], [ANY] + [VMEM] * 4, 0, block)(
            done, whole, *got
        )
    with jax.named_scope("text"):
        (text_grad,) = call(
            text_sum, [shape(f32, ROWS, WIDTH)], [ANY, SMEM] + [VMEM] * 4, 0, block * 16
        )(whole_send, valid_count, terms, u1, u2, u3)
    return hidden_grad, weight_grad, text_grad


def solution(mesh):
    fine = Mesh(mesh.devices.reshape(4, 2, 2, 4, 2, 2), AXES)
    blk = ("zh", "x1", "x0", "y", "c")
    by_row = P(("zl",) + blk, None)
    return jax.shard_map(
        per_device,
        mesh=fine,
        in_specs=(by_row, P(), by_row, P("zl", None), P(("zl",) + blk), P(), P()),
        out_specs=(by_row, P(blk, None), by_row),
        check_vma=False,
    )
```

```python
import jax
import jax.numpy as jnp
from jax import lax
from jax.experimental import pallas as pl
from jax.experimental.pallas import tpu as pltpu
from jax.sharding import Mesh, PartitionSpec as P

epsilon = 1e-06
AXES = ("zh", "x1", "x0", "y", "c", "zl")
f32 = jnp.float32
bf16 = jnp.bfloat16
ROWS = 128
WIDTH = 1152
VMEM = pl.BlockSpec(memory_space=pltpu.VMEM)
SMEM = pl.BlockSpec(memory_space=pltpu.SMEM)
ANY = pl.BlockSpec(memory_space=pl.ANY)
HBM = pl.BlockSpec(memory_space=pltpu.HBM)


def dot(a, b, ca, cb):
    return lax.dot_general(a, b, (((ca,), (cb,)), ((), ())), preferred_element_type=f32)


def xor(x, axis, step):
    size = lax.axis_size(axis)
    return lax.ppermute(x, axis, [(i, i ^ step) for i in range(size)])


def shape(dtype, *dims):
    return jax.ShapeDtypeStruct(dims, dtype)


def in_hbm(x):
    return pltpu.with_memory_space_constraint(x, pltpu.HBM)


def call(body, outs, specs, flops, moved, scratch=(), vmem=8):
    return pl.pallas_call(
        body,
        out_shape=outs,
        in_specs=specs,
        out_specs=[VMEM] * len(outs),
        scratch_shapes=scratch,
        compiler_params=pltpu.CompilerParams(vmem_limit_bytes=vmem << 20),
        cost_estimate=pl.CostEstimate(flops=flops, bytes_accessed=moved, transcendentals=0),
    )


def prepare(count, hidden, text, hid_out, txt_out, hid_in, txt_in, sems):
    copies = [
        pltpu.make_async_copy(text, txt_in, sems.at[0]),
        pltpu.make_async_copy(hidden, hid_in, sems.at[1]),
    ]
    for copy in copies:
        copy.start()
    keep = lax.broadcasted_iota(jnp.int32, (ROWS, 1), 0) < count[0]
    copies[0].wait()
    txt = txt_in[...].astype(f32)
    txt = txt * lax.rsqrt(jnp.sum(txt * txt, axis=1, keepdims=True) + epsilon)
    txt_out[...] = jnp.where(keep, txt, 0.0).astype(bf16)
    copies[1].wait()
    hid_out[...] = jnp.where(keep, hid_in[...].astype(f32), 0.0).astype(bf16)


def join(after, own, paired, t1, t3, both, first, second):
    both[:ROWS] = own[...]
    both[ROWS:] = paired[...]
    first[...] = t3[: ROWS // 2]
    second[...] = t1[ROWS // 2 :]


def ahead(after, pair_ids, weight, held, chosen, left, right, sem):
    copy = pltpu.make_async_copy(weight, held, sem)
    copy.start()
    zh, x1, x0, y, c, zl = (lax.axis_index(a) for a in AXES)
    row = lax.broadcasted_iota(jnp.int32, (576, 1), 0)
    k, row = row // 144, row % 144
    j, row = row // 36, row % 36
    m, r = row // 9, row % 9
    turn = jnp.where(zl == 0, 4 - m, m)
    owner = (zh + turn) % 4
    place = owner * 288 + (k ^ (x1 * 2 + x0)) * 72 + (j ^ y) * 18 + c * 9 + r
    spots = lax.broadcasted_iota(jnp.int32, (576, WIDTH), 1)
    chosen[...] = (spots == place).astype(f32).astype(bf16)
    base = (zh * 2 + x1) * 16

    def label(px, py, pc):
        start = pl.multiple_of((base + (px * 4 + py) * 2 + pc) * ROWS, ROWS)
        return pair_ids[:, pl.ds(start, ROWS)]

    for k, (px, pc) in enumerate(((x0, c), (1 - x0, c), (x0, 1 - c), (1 - x0, 1 - c))):
        tall = jnp.transpose(jnp.broadcast_to(label(px, y, pc), (8, ROWS)))
        left[k * ROWS : (k + 1) * ROWS, :] = tall[:, :1]
    for j in range(4):
        right[:, j * ROWS : (j + 1) * ROWS] = label(x0, y ^ j, c)
    copy.wait()


def project(both, cores, weight, chosen, embed, normed, inverse, turned):
    hid = jnp.concatenate([both[...], cores[...]], 0)
    projected = dot(hid, weight[...], 1, 0)
    turned[...] = dot(chosen[...], hid, 1, 1).astype(bf16)
    inv = lax.rsqrt(jnp.sum(projected * projected, axis=1, keepdims=True) + epsilon)
    unit = projected * inv
    normed[...] = unit
    embed[...] = unit.astype(bf16)
    inverse[...] = inv


def tile(scale, bias, left, right, embed, normed, inverse, t0, t1, t2a, t2b, t3, coef_out, part_out, part_send):
    txt = jnp.concatenate([t0[...], t1[...], t2a[...], t2b[...], t3[...]], 0)
    scores = scale[0] * dot(embed[...], txt, 1, 1) + bias[0]
    target = jnp.where(left[...] == right[...], 1.0, -1.0).astype(f32)
    coef = (-target * jax.nn.sigmoid(-target * scores) * scale[0]).astype(bf16)
    coef_out[...] = coef
    grad = dot(coef, txt, 1, 0)
    unit = normed[...]
    radial = jnp.sum(unit * grad, axis=1, keepdims=True)
    part = (grad - unit * radial) * inverse[...]
    part_out[...] = part
    part_send[...] = part.astype(bf16)


def text_terms(coef, embed, terms):
    terms[...] = dot(coef[...], embed[...], 0, 0)


def weight_terms(part, arrived, turned, terms, rows, own, s1, s2, s3, t1, t2):
    half = 2 * ROWS
    top = part[:half] + arrived[half:].astype(f32)
    low = part[half:] + arrived[:half].astype(f32)
    rows[...] = top
    grad = dot(turned[...], jnp.concatenate([top, low], 0).astype(bf16), 1, 0)
    own[...] = grad[:144]
    for k, out in enumerate((s1, s2, s3)):
        out[...] = grad[(k + 1) * 144 : (k + 2) * 144].astype(bf16)
    for k, out in enumerate((t1, t2)):
        out[...] = terms[(k + 1) * ROWS : (k + 2) * ROWS].astype(bf16)


def first_sum(own, a1, a2, a3, b1, b2, out, s1, s2, s3, held):
    held[...] = own[...] + a2[...].astype(f32) + a1[...].astype(f32) + a3[...].astype(f32)
    out[...] = held[:36]
    for k, send in enumerate((s1, s2, s3)):
        send[...] = held[(k + 1) * 36 : (k + 2) * 36].astype(bf16)


def second_sum(own, a1, a2, a3, rows, terms, send, rows_send, t3):
    total = own[...] + a2[...].astype(f32) + a1[...].astype(f32) + a3[...].astype(f32)
    send[...] = total.astype(bf16)
    rows_send[...] = rows[ROWS:].astype(bf16)
    t3[...] = terms[3 * ROWS :].astype(bf16)


def third_sum(own, arrived, out, near, far, mine, held):
    mine[...] = own[...].astype(f32)
    held[...] = arrived[...].astype(f32)
    out[...] = mine[:9] + held[:9]
    near[...] = mine[9:18] + held[27:36]
    far[...] = mine[18:27] + held[18:27]


def last_sum(after, own, a1, a2, a3, out):
    out[...] = own[...] + (a1[...] + a2[...]) + a3[...]


def text_sum(after, count, terms, b1, b2, b3, out):
    keep = lax.broadcasted_iota(jnp.int32, (ROWS, 1), 0) < count[0]
    total = terms[:ROWS] + b2[...].astype(f32) + b1[...].astype(f32) + b3[...].astype(f32)
    out[...] = jnp.where(keep, total, 0.0)


def back(count, rows, arrived, weight, out, done):
    total = (rows[:ROWS] + arrived[...].astype(f32)).astype(bf16)
    grad = dot(total, weight[...], 1, 1)
    keep = lax.broadcasted_iota(jnp.int32, (ROWS, 1), 0) < count[0]
    out[...] = jnp.where(keep, grad, 0.0).astype(bf16)
    done[...] = jnp.zeros((8, ROWS), f32)


def per_device(hidden, weight, text, pair_ids, valid_count, logit_scale, logit_bias):
    X = ("x1", "x0")
    block = ROWS * WIDTH
    wide, tall = shape(bf16, ROWS, WIDTH), shape(f32, 512, WIDTH)
    with jax.named_scope("prepare"):
        hid, txt = call(
            prepare,
            [wide, wide],
            [SMEM, HBM, HBM],
            0,
            block,
            [pltpu.VMEM((ROWS, WIDTH), bf16)] * 2 + [pltpu.SemaphoreType.DMA((2,))],
        )(valid_count, in_hbm(hidden), in_hbm(text))
    with jax.named_scope("gather"):
        hid_x = xor(hid, "x0", 1)
        txt_1 = xor(txt, "y", 1)
        txt_3 = xor(txt, "y", 3)
        held, chosen, left, right = call(
            ahead,
            [
                shape(bf16, WIDTH, WIDTH),
                shape(bf16, 576, WIDTH),
                shape(jnp.int32, 512, 1),
                shape(jnp.int32, 1, 512),
            ],
            [ANY, VMEM, HBM],
            block * 1000,
            block,
            [pltpu.SemaphoreType.DMA],
        )(hid, pair_ids, in_hbm(weight))
        both, first, second = call(
            join,
            [shape(bf16, 256, WIDTH)] + [shape(bf16, 64, WIDTH)] * 2,
            [ANY] + [VMEM] * 4,
            0,
            block,
        )(chosen, hid, hid_x, txt_1, txt_3)
        hid_c = xor(both, "c", 1)
        txt_2a = xor(first, "y", 1)
        txt_2b = xor(second, "y", 3)
    with jax.named_scope("project"):
        embed, normed, inverse, turned = call(
            project,
            [shape(bf16, 512, WIDTH), tall, shape(f32, 512, 1), shape(bf16, 576, 512)],
            [VMEM] * 4,
            0,
            block,
            vmem=16,
        )(both, hid_c, held, chosen)
    with jax.named_scope("tile"):
        coef, part, part_send = call(
            tile,
            [shape(bf16, 512, 512), tall, shape(bf16, 512, WIDTH)],
            [SMEM, SMEM] + [VMEM] * 10,
            0,
            block,
            vmem=16,
        )(
            logit_scale.reshape(1), logit_bias.reshape(1), left, right,
            embed, normed, inverse, txt, txt_1, txt_2a, txt_2b, txt_3,
        )
    with jax.named_scope("core"):
        arrived = xor(part_send, "c", 1)
    with jax.named_scope("text"):
        (terms,) = call(text_terms, [tall], [VMEM] * 2, 0, block)(coef, embed)
    with jax.named_scope("weight"):
        rows, own, s1, s2, s3, u1, u2 = call(
            weight_terms,
            [shape(f32, 256, WIDTH), shape(f32, 144, WIDTH)]
            + [shape(bf16, 144, WIDTH)] * 3
            + [wide] * 2,
            [VMEM] * 4,
            0,
            block,
            vmem=16,
        )(part, arrived, turned, terms)
        s2, s1, s3 = xor(s2, X, 2), xor(s1, X, 1), xor(s3, X, 3)
        u2, u1 = xor(u2, "y", 2), xor(u1, "y", 1)
        small, small_b = shape(f32, 36, WIDTH), shape(bf16, 36, WIDTH)
        whole, s1, s2, s3 = call(
            first_sum,
            [small] + [small_b] * 3,
            [VMEM] * 4 + [ANY] * 2,
            0,
            block,
            [pltpu.VMEM((144, WIDTH), f32)],
        )(own, s1, s2, s3, u1, u2)
        s2, s1, s3 = xor(s2, "y", 2), xor(s1, "y", 1), xor(s3, "y", 3)
        whole_send, rows_send, u3 = call(
            second_sum, [small_b, wide, wide], [VMEM] * 6, 0, block
        )(whole, s1, s2, s3, rows, terms)
        u3 = xor(u3, "y", 3)
        arrived = xor(whole_send, "zl", 1)
        whole, near, far = call(
            third_sum,
            [shape(f32, 9, WIDTH)] * 3,
            [VMEM] * 2,
            0,
            block,
            [pltpu.VMEM((36, WIDTH), f32)] * 2,
        )(whole_send, arrived)
        Z = ("zh", "zl")
        steps = (near, 1), (near, 2), (far, 3)
        got = [
            lax.ppermute(x, Z, [(p, (p + (hop if p % 2 else -hop)) % 8) for p in range(8)])
            for x, hop in steps
        ]
    with jax.named_scope("hidden"):
        rows_x = xor(rows_send, "x0", 1)
        hidden_grad, done = call(
            back, [wide, shape(f32, 8, ROWS)], [SMEM] + [VMEM] * 3, 2 * block * WIDTH, WIDTH * WIDTH * 2
        )(valid_count, rows, rows_x, held)
    with jax.named_scope("weight"):
        (weight_grad,) = call(last_sum, [shape(f32, 9, WIDTH)], [ANY] + [VMEM] * 4, 0, block)(
            done, whole, *got
        )
    with jax.named_scope("text"):
        (text_grad,) = call(
            text_sum, [shape(f32, ROWS, WIDTH)], [ANY, SMEM] + [VMEM] * 4, 0, block * 16
        )(whole_send, valid_count, terms, u1, u2, u3)
    return hidden_grad, weight_grad, text_grad


def solution(mesh):
    fine = Mesh(mesh.devices.reshape(4, 2, 2, 4, 2, 2), AXES)
    blk = ("zh", "x1", "x0", "y", "c")
    by_row = P(("zl",) + blk, None)
    return jax.shard_map(
        per_device,
        mesh=fine,
        in_specs=(by_row, P(), by_row, P("zl", None), P(("zl",) + blk), P(), P()),
        out_specs=(by_row, P(blk, None), by_row),
        check_vma=False,
    )
```

```python
import jax
import jax.numpy as jnp
from jax import lax
from jax.experimental import pallas as pl
from jax.experimental.pallas import tpu as pltpu
from jax.sharding import Mesh, PartitionSpec as P

epsilon = 1e-06
AXES = ("zh", "x1", "x0", "y", "c", "zl")
f32 = jnp.float32
bf16 = jnp.bfloat16
ROWS = 128
WIDTH = 1152
VMEM = pl.BlockSpec(memory_space=pltpu.VMEM)
SMEM = pl.BlockSpec(memory_space=pltpu.SMEM)
ANY = pl.BlockSpec(memory_space=pl.ANY)
HBM = pl.BlockSpec(memory_space=pltpu.HBM)


def dot(a, b, ca, cb):
    return lax.dot_general(a, b, (((ca,), (cb,)), ((), ())), preferred_element_type=f32)


def xor(x, axis, step):
    size = lax.axis_size(axis)
    return lax.ppermute(x, axis, [(i, i ^ step) for i in range(size)])


def shape(dtype, *dims):
    return jax.ShapeDtypeStruct(dims, dtype)


def in_hbm(x):
    return pltpu.with_memory_space_constraint(x, pltpu.HBM)


def call(body, outs, specs, flops, moved, scratch=(), vmem=8):
    return pl.pallas_call(
        body,
        out_shape=outs,
        in_specs=specs,
        out_specs=[VMEM] * len(outs),
        scratch_shapes=scratch,
        compiler_params=pltpu.CompilerParams(vmem_limit_bytes=vmem << 20),
        cost_estimate=pl.CostEstimate(flops=flops, bytes_accessed=moved, transcendentals=0),
    )


def prepare(count, hidden, text, hid_out, txt_out, hid_in, txt_in, sems):
    copies = [
        pltpu.make_async_copy(text, txt_in, sems.at[0]),
        pltpu.make_async_copy(hidden, hid_in, sems.at[1]),
    ]
    for copy in copies:
        copy.start()
    keep = lax.broadcasted_iota(jnp.int32, (ROWS, 1), 0) < count[0]
    copies[0].wait()
    txt = txt_in[...].astype(f32)
    txt = txt * lax.rsqrt(jnp.sum(txt * txt, axis=1, keepdims=True) + epsilon)
    txt_out[...] = jnp.where(keep, txt, 0.0).astype(bf16)
    copies[1].wait()
    hid_out[...] = jnp.where(keep, hid_in[...].astype(f32), 0.0).astype(bf16)


def join(after, own, paired, t1, t3, both, first, second):
    both[:ROWS] = own[...]
    both[ROWS:] = paired[...]
    first[...] = t3[: ROWS // 2]
    second[...] = t1[ROWS // 2 :]


def ahead(after, scale, bias, pair_ids, weight, held, chosen, left, right, settings, sem):
    copy = pltpu.make_async_copy(weight, held, sem)
    copy.start()
    settings[0:1, :] = jnp.full((1, ROWS), scale[0], f32)
    settings[1:2, :] = jnp.full((1, ROWS), bias[0], f32)
    zh, x1, x0, y, c, zl = (lax.axis_index(a) for a in AXES)
    row = lax.broadcasted_iota(jnp.int32, (576, 1), 0)
    k, row = row // 144, row % 144
    j, row = row // 36, row % 36
    m, r = row // 9, row % 9
    turn = jnp.where(zl == 0, 4 - m, m)
    owner = (zh + turn) % 4
    core = (c + owner + zh) % 2
    place = owner * 288 + (k ^ (x1 * 2 + x0)) * 72 + (j ^ y) * 18 + core * 9 + r
    spots = lax.broadcasted_iota(jnp.int32, (576, WIDTH), 1)
    chosen[...] = (spots == place).astype(f32).astype(bf16)
    base = (zh * 2 + x1) * 16

    def label(px, py, pc):
        start = pl.multiple_of((base + (px * 4 + py) * 2 + pc) * ROWS, ROWS)
        return pair_ids[:, pl.ds(start, ROWS)]

    for k, (px, pc) in enumerate(((x0, c), (1 - x0, c), (x0, 1 - c), (1 - x0, 1 - c))):
        tall = jnp.transpose(jnp.broadcast_to(label(px, y, pc), (8, ROWS)))
        left[k * ROWS : (k + 1) * ROWS, :] = tall[:, :1]
    for j in range(4):
        right[:, j * ROWS : (j + 1) * ROWS] = label(x0, y ^ j, c)
    copy.wait()


def project(both, cores, weight, chosen, embed, normed, inverse, turned):
    hid = jnp.concatenate([both[...], cores[...]], 0)
    projected = dot(hid, weight[...], 1, 0)
    turned[...] = dot(chosen[...], hid, 1, 1).astype(bf16)
    inv = lax.rsqrt(jnp.sum(projected * projected, axis=1, keepdims=True) + epsilon)
    unit = projected * inv
    normed[...] = unit
    embed[...] = unit.astype(bf16)
    inverse[...] = inv


def tile(settings, left, right, embed, normed, inverse, t0, t1, t2a, t2b, t3, coef_out, part_out, part_send):
    txt = jnp.concatenate([t0[...], t1[...], t2a[...], t2b[...], t3[...]], 0)
    scale, bias = settings[0:1, 0:1], settings[1:2, 0:1]
    scores = scale * dot(embed[...], txt, 1, 1) + bias
    target = jnp.where(left[...] == right[...], 1.0, -1.0).astype(f32)
    coef = (-target * jax.nn.sigmoid(-target * scores) * scale).astype(bf16)
    coef_out[...] = coef
    grad = dot(coef, txt, 1, 0)
    unit = normed[...]
    radial = jnp.sum(unit * grad, axis=1, keepdims=True)
    part = (grad - unit * radial) * inverse[...]
    part_out[...] = part
    part_send[...] = part.astype(bf16)


def text_terms(coef, embed, terms, t2):
    grad = dot(coef[...], embed[...], 0, 0)
    terms[...] = grad
    t2[...] = grad[2 * ROWS : 3 * ROWS].astype(bf16)


def weight_terms(part, arrived, turned, terms, rows, own, s1, s2, s3, t1, t3):
    half = 2 * ROWS
    top = part[:half] + arrived[half:].astype(f32)
    low = part[half:] + arrived[:half].astype(f32)
    rows[...] = top
    grad = dot(turned[...], jnp.concatenate([top, low], 0).astype(bf16), 1, 0)
    own[...] = grad[:144]
    for k, out in enumerate((s1, s2, s3)):
        out[...] = grad[(k + 1) * 144 : (k + 2) * 144].astype(bf16)
    t1[...] = terms[ROWS : 2 * ROWS].astype(bf16)
    t3[...] = terms[3 * ROWS :].astype(bf16)


def first_sum(own, a1, a2, a3, b1, b2, b3, out, s1, s2, s3, held):
    held[...] = own[...] + a2[...].astype(f32) + a1[...].astype(f32) + a3[...].astype(f32)
    out[...] = held[:36]
    for k, send in enumerate((s1, s2, s3)):
        send[...] = held[(k + 1) * 36 : (k + 2) * 36].astype(bf16)


def second_sum(own, a1, a2, a3, rows, send, rows_send):
    total = own[...] + a2[...].astype(f32) + a1[...].astype(f32) + a3[...].astype(f32)
    send[...] = total.astype(bf16)
    rows_send[...] = rows[ROWS:].astype(bf16)


def third_sum(own, arrived, out, near, far, mine, held):
    mine[...] = own[...].astype(f32)
    held[...] = arrived[...].astype(f32)
    out[...] = mine[:9] + held[:9]
    near[...] = mine[9:18] + held[27:36]
    far[...] = mine[18:27] + held[18:27]


def last_sum(after, own, a1, a2, a3, out):
    out[...] = own[...] + (a1[...] + a2[...]) + a3[...]


def text_sum(after, count, terms, b1, b2, b3, out):
    keep = lax.broadcasted_iota(jnp.int32, (ROWS, 1), 0) < count[0]
    total = terms[:ROWS] + b2[...].astype(f32) + b1[...].astype(f32) + b3[...].astype(f32)
    out[...] = jnp.where(keep, total, 0.0)


def back(count, rows, arrived, weight, out, done):
    total = (rows[:ROWS] + arrived[...].astype(f32)).astype(bf16)
    grad = dot(total, weight[...], 1, 1)
    keep = lax.broadcasted_iota(jnp.int32, (ROWS, 1), 0) < count[0]
    out[...] = jnp.where(keep, grad, 0.0).astype(bf16)
    done[...] = jnp.zeros((8, ROWS), f32)


def along_z(x, hop, cross):
    pairs = []
    for z in range(8):
        to = (z + (hop if z % 2 else -hop)) % 8
        for c in range(2):
            pairs.append((z // 2 * 4 + c * 2 + z % 2, to // 2 * 4 + (c ^ cross) * 2 + to % 2))
    return lax.ppermute(x, ("zh", "c", "zl"), pairs)


def per_device(hidden, weight, text, pair_ids, valid_count, logit_scale, logit_bias):
    X = ("x1", "x0")
    block = ROWS * WIDTH
    wide, tall = shape(bf16, ROWS, WIDTH), shape(f32, 512, WIDTH)
    with jax.named_scope("prepare"):
        hid, txt = call(
            prepare,
            [wide, wide],
            [SMEM, HBM, HBM],
            0,
            block,
            [pltpu.VMEM((ROWS, WIDTH), bf16)] * 2 + [pltpu.SemaphoreType.DMA((2,))],
        )(valid_count, in_hbm(hidden), in_hbm(text))
    with jax.named_scope("gather"):
        hid_x = xor(hid, "x0", 1)
        txt_1 = xor(txt, "y", 1)
        txt_3 = xor(txt, "y", 3)
        held, chosen, left, right, settings = call(
            ahead,
            [
                shape(bf16, WIDTH, WIDTH),
                shape(bf16, 576, WIDTH),
                shape(jnp.int32, 512, 1),
                shape(jnp.int32, 1, 512),
                shape(f32, 2, ROWS),
            ],
            [ANY, SMEM, SMEM, VMEM, HBM],
            block * 1000,
            block,
            [pltpu.SemaphoreType.DMA],
        )(hid, logit_scale.reshape(1), logit_bias.reshape(1), pair_ids, in_hbm(weight))
        both, first, second = call(
            join,
            [shape(bf16, 256, WIDTH)] + [shape(bf16, 64, WIDTH)] * 2,
            [ANY] + [VMEM] * 4,
            0,
            block,
        )(chosen, hid, hid_x, txt_1, txt_3)
        hid_c = xor(both, "c", 1)
        txt_2a = xor(first, "y", 1)
        txt_2b = xor(second, "y", 3)
    with jax.named_scope("project"):
        embed, normed, inverse, turned = call(
            project,
            [shape(bf16, 512, WIDTH), tall, shape(f32, 512, 1), shape(bf16, 576, 512)],
            [VMEM] * 4,
            0,
            block,
            vmem=16,
        )(both, hid_c, held, chosen)
    with jax.named_scope("tile"):
        coef, part, part_send = call(
            tile,
            [shape(bf16, 512, 512), tall, shape(bf16, 512, WIDTH)],
            [VMEM] * 11,
            0,
            block,
            vmem=16,
        )(
            settings, left, right, embed, normed, inverse, txt, txt_1, txt_2a, txt_2b, txt_3,
        )
    with jax.named_scope("core"):
        arrived = xor(part_send, "c", 1)
    with jax.named_scope("text"):
        terms, u2 = call(text_terms, [tall, wide], [VMEM] * 2, 0, block)(coef, embed)
        u2 = xor(u2, "y", 2)
    with jax.named_scope("weight"):
        rows, own, s1, s2, s3, u1, u3 = call(
            weight_terms,
            [shape(f32, 256, WIDTH), shape(f32, 144, WIDTH)]
            + [shape(bf16, 144, WIDTH)] * 3
            + [wide] * 2,
            [VMEM] * 4,
            0,
            block,
            vmem=16,
        )(part, arrived, turned, terms)
        s2, s1, s3 = xor(s2, X, 2), xor(s1, X, 1), xor(s3, X, 3)
        u1, u3 = xor(u1, "y", 1), xor(u3, "y", 3)
        small, small_b = shape(f32, 36, WIDTH), shape(bf16, 36, WIDTH)
        whole, s1, s2, s3 = call(
            first_sum,
            [small] + [small_b] * 3,
            [VMEM] * 4 + [ANY] * 3,
            0,
            block,
            [pltpu.VMEM((144, WIDTH), f32)],
        )(own, s1, s2, s3, u1, u2, u3)
        s2, s1, s3 = xor(s2, "y", 2), xor(s1, "y", 1), xor(s3, "y", 3)
        whole_send, rows_send = call(second_sum, [small_b, wide], [VMEM] * 5, 0, block)(
            whole, s1, s2, s3, rows
        )
        arrived = xor(whole_send, "zl", 1)
        whole, near, far = call(
            third_sum,
            [shape(f32, 9, WIDTH)] * 3,
            [VMEM] * 2,
            0,
            block,
            [pltpu.VMEM((36, WIDTH), f32)] * 2,
        )(whole_send, arrived)
        got = [along_z(near, 1, 1), along_z(near, 2, 1), along_z(far, 3, 0)]
    with jax.named_scope("hidden"):
        rows_x = xor(rows_send, "x0", 1)
        hidden_grad, done = call(
            back, [wide, shape(f32, 8, ROWS)], [SMEM] + [VMEM] * 3, 2 * block * WIDTH, WIDTH * WIDTH * 2
        )(valid_count, rows, rows_x, held)
    with jax.named_scope("weight"):
        (weight_grad,) = call(last_sum, [shape(f32, 9, WIDTH)], [ANY] + [VMEM] * 4, 0, block)(
            done, whole, *got
        )
    with jax.named_scope("text"):
        (text_grad,) = call(
            text_sum, [shape(f32, ROWS, WIDTH)], [ANY, SMEM] + [VMEM] * 4, 0, block * 16
        )(whole_send, valid_count, terms, u1, u2, u3)
    return hidden_grad, weight_grad, text_grad


def solution(mesh):
    fine = Mesh(mesh.devices.reshape(4, 2, 2, 4, 2, 2), AXES)
    blk = ("zh", "x1", "x0", "y", "c")
    by_row = P(("zl",) + blk, None)
    return jax.shard_map(
        per_device,
        mesh=fine,
        in_specs=(by_row, P(), by_row, P("zl", None), P(("zl",) + blk), P(), P()),
        out_specs=(by_row, P(blk, None), by_row),
        check_vma=False,
    )
```

```python
import jax
import jax.numpy as jnp
from jax import lax
from jax.experimental import pallas as pl
from jax.experimental.pallas import tpu as pltpu
from jax.sharding import Mesh, PartitionSpec as P

epsilon = 1e-06
AXES = ("zh", "x1", "x0", "y", "c", "zl")
f32 = jnp.float32
bf16 = jnp.bfloat16
ROWS = 128
WIDTH = 1152
VMEM = pl.BlockSpec(memory_space=pltpu.VMEM)
SMEM = pl.BlockSpec(memory_space=pltpu.SMEM)
ANY = pl.BlockSpec(memory_space=pl.ANY)
HBM = pl.BlockSpec(memory_space=pltpu.HBM)


def dot(a, b, ca, cb):
    return lax.dot_general(a, b, (((ca,), (cb,)), ((), ())), preferred_element_type=f32)


def xor(x, axis, step):
    size = lax.axis_size(axis)
    return lax.ppermute(x, axis, [(i, i ^ step) for i in range(size)])


def shape(dtype, *dims):
    return jax.ShapeDtypeStruct(dims, dtype)


def in_hbm(x):
    return pltpu.with_memory_space_constraint(x, pltpu.HBM)


def call(body, outs, specs, flops, moved, scratch=(), vmem=8):
    return pl.pallas_call(
        body,
        out_shape=outs,
        in_specs=specs,
        out_specs=[VMEM] * len(outs),
        scratch_shapes=scratch,
        compiler_params=pltpu.CompilerParams(vmem_limit_bytes=vmem << 20),
        cost_estimate=pl.CostEstimate(flops=flops, bytes_accessed=moved, transcendentals=0),
    )


def prepare(count, hidden, text, hid_out, txt_out, hid_in, txt_in, sems):
    copies = [
        pltpu.make_async_copy(text, txt_in, sems.at[0]),
        pltpu.make_async_copy(hidden, hid_in, sems.at[1]),
    ]
    for copy in copies:
        copy.start()
    keep = lax.broadcasted_iota(jnp.int32, (ROWS, 1), 0) < count[0]
    copies[0].wait()
    txt = txt_in[...].astype(f32)
    txt = txt * lax.rsqrt(jnp.sum(txt * txt, axis=1, keepdims=True) + epsilon)
    txt_out[...] = jnp.where(keep, txt, 0.0).astype(bf16)
    copies[1].wait()
    hid_out[...] = jnp.where(keep, hid_in[...].astype(f32), 0.0).astype(bf16)


def join(after, own, paired, t1, t3, both, first, second):
    both[:ROWS] = own[...]
    both[ROWS:] = paired[...]
    first[...] = t3[: ROWS // 2]
    second[...] = t1[ROWS // 2 :]


def ahead(after, scale, bias, pair_ids, weight, held, chosen, left, right, settings, sem):
    copy = pltpu.make_async_copy(weight, held, sem)
    copy.start()
    settings[0:1, :] = jnp.full((1, ROWS), scale[0], f32)
    settings[1:2, :] = jnp.full((1, ROWS), bias[0], f32)
    zh, x1, x0, y, c, zl = (lax.axis_index(a) for a in AXES)
    row = lax.broadcasted_iota(jnp.int32, (576, 1), 0)
    k, row = row // 144, row % 144
    j, row = row // 36, row % 36
    m, r = row // 9, row % 9
    turn = jnp.where(zl == 0, 4 - m, m)
    owner = (zh + turn) % 4
    core = (c + owner + zh) % 2
    place = owner * 288 + (k ^ (x1 * 2 + x0)) * 72 + (j ^ y) * 18 + core * 9 + r
    spots = lax.broadcasted_iota(jnp.int32, (576, WIDTH), 1)
    chosen[...] = (spots == place).astype(f32).astype(bf16)
    base = (zh * 2 + x1) * 16

    def label(px, py, pc):
        start = pl.multiple_of((base + (px * 4 + py) * 2 + pc) * ROWS, ROWS)
        return pair_ids[:, pl.ds(start, ROWS)]

    for k, (px, pc) in enumerate(((x0, c), (1 - x0, c), (x0, 1 - c), (1 - x0, 1 - c))):
        tall = jnp.transpose(jnp.broadcast_to(label(px, y, pc), (8, ROWS)))
        left[k * ROWS : (k + 1) * ROWS, :] = tall[:, :1]
    for j in range(4):
        right[:, j * ROWS : (j + 1) * ROWS] = label(x0, y ^ j, c)
    copy.wait()


def project(both, cores, weight, chosen, embed, normed, inverse, turned):
    hid = jnp.concatenate([both[...], cores[...]], 0)
    projected = dot(hid, weight[...], 1, 0)
    turned[...] = dot(chosen[...], hid, 1, 1).astype(bf16)
    inv = lax.rsqrt(jnp.sum(projected * projected, axis=1, keepdims=True) + epsilon)
    unit = projected * inv
    normed[...] = unit
    embed[...] = unit.astype(bf16)
    inverse[...] = inv


def tile(settings, left, right, embed, normed, inverse, t0, t1, t2a, t2b, t3, coef_out, part_out, part_send):
    txt = jnp.concatenate([t0[...], t1[...], t2a[...], t2b[...], t3[...]], 0)
    scale, bias = settings[0:1, 0:1], settings[1:2, 0:1]
    scores = scale * dot(embed[...], txt, 1, 1) + bias
    target = jnp.where(left[...] == right[...], 1.0, -1.0).astype(f32)
    coef = (-target * jax.nn.sigmoid(-target * scores) * scale).astype(bf16)
    coef_out[...] = coef
    grad = dot(coef, txt, 1, 0)
    unit = normed[...]
    radial = jnp.sum(unit * grad, axis=1, keepdims=True)
    part = (grad - unit * radial) * inverse[...]
    part_out[...] = part
    part_send[...] = part.astype(bf16)


def text_terms(coef, embed, terms, t2):
    grad = dot(coef[...], embed[...], 0, 0)
    terms[...] = grad
    t2[...] = grad[2 * ROWS : 3 * ROWS].astype(bf16)


def weight_terms(part, arrived, turned, terms, rows, own, s1, s2, s3, t1, t3):
    half = 2 * ROWS
    top = part[:half] + arrived[half:].astype(f32)
    low = part[half:] + arrived[:half].astype(f32)
    rows[...] = top
    grad = dot(turned[...], jnp.concatenate([top, low], 0).astype(bf16), 1, 0)
    own[...] = grad[:144]
    for k, out in enumerate((s1, s2, s3)):
        out[...] = grad[(k + 1) * 144 : (k + 2) * 144].astype(bf16)
    t1[...] = terms[ROWS : 2 * ROWS].astype(bf16)
    t3[...] = terms[3 * ROWS :].astype(bf16)


def first_sum(own, a2, a1, a3, b1, b2, b3, out, s1, s2, s3, held):
    held[...] = own[...] + a2[...].astype(f32) + a1[...].astype(f32) + a3[...].astype(f32)
    out[...] = held[:36]
    for k, send in enumerate((s1, s2, s3)):
        send[...] = held[(k + 1) * 36 : (k + 2) * 36].astype(bf16)


def second_sum(own, a2, a1, a3, rows, keep, send, rows_send, held):
    total = own[...] + a2[...].astype(f32) + a1[...].astype(f32) + a3[...].astype(f32)
    total = total.astype(bf16).astype(f32)
    held[...] = total
    keep[...] = total
    send[...] = jnp.concatenate([held[:9], held[18:]], 0).astype(bf16)
    rows_send[...] = rows[ROWS:].astype(bf16)


def third_sum(own, arrived, out, near, far, held):
    held[...] = arrived[...].astype(f32)
    out[...] = own[:9] + held[:9]
    near[...] = (own[9:18] + held[18:]).astype(bf16)
    far[...] = (own[18:27] + held[9:18]).astype(bf16)


def last_sum(after, own, a1, a3, a2, out):
    sides = a1[...].astype(f32) + a2[...].astype(f32)
    out[...] = own[...] + sides + a3[...].astype(f32)


def text_sum(after, count, terms, b1, b2, b3, out):
    keep = lax.broadcasted_iota(jnp.int32, (ROWS, 1), 0) < count[0]
    total = terms[:ROWS] + b2[...].astype(f32) + b1[...].astype(f32) + b3[...].astype(f32)
    out[...] = jnp.where(keep, total, 0.0)


def back(count, rows, arrived, weight, out, done):
    total = (rows[:ROWS] + arrived[...].astype(f32)).astype(bf16)
    grad = dot(total, weight[...], 1, 1)
    keep = lax.broadcasted_iota(jnp.int32, (ROWS, 1), 0) < count[0]
    out[...] = jnp.where(keep, grad, 0.0).astype(bf16)
    done[...] = jnp.zeros((8, ROWS), f32)


def along_z(x, hop, cross):
    pairs = []
    for z in range(8):
        to = (z + (hop if z % 2 else -hop)) % 8
        for c in range(2):
            pairs.append((z // 2 * 4 + c * 2 + z % 2, to // 2 * 4 + (c ^ cross) * 2 + to % 2))
    return lax.ppermute(x, ("zh", "c", "zl"), pairs)


def per_device(hidden, weight, text, pair_ids, valid_count, logit_scale, logit_bias):
    X = ("x1", "x0")
    block = ROWS * WIDTH
    wide, tall = shape(bf16, ROWS, WIDTH), shape(f32, 512, WIDTH)
    with jax.named_scope("prepare"):
        hid, txt = call(
            prepare,
            [wide, wide],
            [SMEM, HBM, HBM],
            0,
            block,
            [pltpu.VMEM((ROWS, WIDTH), bf16)] * 2 + [pltpu.SemaphoreType.DMA((2,))],
        )(valid_count, in_hbm(hidden), in_hbm(text))
    with jax.named_scope("gather"):
        hid_x = xor(hid, "x0", 1)
        txt_1 = xor(txt, "y", 1)
        txt_3 = xor(txt, "y", 3)
        held, chosen, left, right, settings = call(
            ahead,
            [
                shape(bf16, WIDTH, WIDTH),
                shape(bf16, 576, WIDTH),
                shape(jnp.int32, 512, 1),
                shape(jnp.int32, 1, 512),
                shape(f32, 2, ROWS),
            ],
            [ANY, SMEM, SMEM, VMEM, HBM],
            block * 1000,
            block,
            [pltpu.SemaphoreType.DMA],
        )(hid, logit_scale.reshape(1), logit_bias.reshape(1), pair_ids, in_hbm(weight))
        both, first, second = call(
            join,
            [shape(bf16, 256, WIDTH)] + [shape(bf16, 64, WIDTH)] * 2,
            [ANY] + [VMEM] * 4,
            0,
            block,
        )(chosen, hid, hid_x, txt_1, txt_3)
        hid_c = xor(both, "c", 1)
        txt_2a = xor(first, "y", 1)
        txt_2b = xor(second, "y", 3)
    with jax.named_scope("project"):
        embed, normed, inverse, turned = call(
            project,
            [shape(bf16, 512, WIDTH), tall, shape(f32, 512, 1), shape(bf16, 576, 512)],
            [VMEM] * 4,
            0,
            block,
            vmem=16,
        )(both, hid_c, held, chosen)
    with jax.named_scope("tile"):
        coef, part, part_send = call(
            tile,
            [shape(bf16, 512, 512), tall, shape(bf16, 512, WIDTH)],
            [VMEM] * 11,
            0,
            block,
            vmem=16,
        )(
            settings, left, right, embed, normed, inverse, txt, txt_1, txt_2a, txt_2b, txt_3,
        )
    with jax.named_scope("core"):
        arrived = xor(part_send, "c", 1)
    with jax.named_scope("text"):
        terms, u2 = call(text_terms, [tall, wide], [VMEM] * 2, 0, block)(coef, embed)
        u2 = xor(u2, "y", 2)
    with jax.named_scope("weight"):
        rows, own, s1, s2, s3, u1, u3 = call(
            weight_terms,
            [shape(f32, 256, WIDTH), shape(f32, 144, WIDTH)]
            + [shape(bf16, 144, WIDTH)] * 3
            + [wide] * 2,
            [VMEM] * 4,
            0,
            block,
            vmem=16,
        )(part, arrived, turned, terms)
        s2, s1, s3 = xor(s2, X, 2), xor(s1, X, 1), xor(s3, X, 3)
        u1, u3 = xor(u1, "y", 1), xor(u3, "y", 3)
        small, small_b = shape(f32, 36, WIDTH), shape(bf16, 36, WIDTH)
        whole, s1, s2, s3 = call(
            first_sum,
            [small] + [small_b] * 3,
            [VMEM] * 4 + [ANY] * 3,
            0,
            block,
            [pltpu.VMEM((144, WIDTH), f32)],
        )(own, s2, s1, s3, u1, u2, u3)
        s2, s1, s3 = xor(s2, "y", 2), xor(s1, "y", 1), xor(s3, "y", 3)
        whole, whole_send, rows_send = call(
            second_sum,
            [small, shape(bf16, 27, WIDTH), wide],
            [VMEM] * 5,
            0,
            block,
            [pltpu.VMEM((36, WIDTH), f32)],
        )(whole, s2, s1, s3, rows)
        arrived = xor(whole_send, "zl", 1)
        whole, near, far = call(
            third_sum,
            [shape(f32, 9, WIDTH)] + [shape(bf16, 9, WIDTH)] * 2,
            [VMEM] * 2,
            0,
            block,
            [pltpu.VMEM((27, WIDTH), f32)],
        )(whole, arrived)
        got = [along_z(near, 1, 1), along_z(far, 3, 0), along_z(near, 2, 1)]
    with jax.named_scope("hidden"):
        rows_x = xor(rows_send, "x0", 1)
        hidden_grad, done = call(
            back, [wide, shape(f32, 8, ROWS)], [SMEM] + [VMEM] * 3, 2 * block * WIDTH, WIDTH * WIDTH * 2
        )(valid_count, rows, rows_x, held)
    with jax.named_scope("weight"):
        (weight_grad,) = call(last_sum, [shape(f32, 9, WIDTH)], [ANY] + [VMEM] * 4, 0, block)(
            done, whole, *got
        )
    with jax.named_scope("text"):
        (text_grad,) = call(
            text_sum, [shape(f32, ROWS, WIDTH)], [ANY, SMEM] + [VMEM] * 4, 0, block * 16
        )(whole_send, valid_count, terms, u1, u2, u3)
    return hidden_grad, weight_grad, text_grad


def solution(mesh):
    fine = Mesh(mesh.devices.reshape(4, 2, 2, 4, 2, 2), AXES)
    blk = ("zh", "x1", "x0", "y", "c")
    by_row = P(("zl",) + blk, None)
    return jax.shard_map(
        per_device,
        mesh=fine,
        in_specs=(by_row, P(), by_row, P("zl", None), P(("zl",) + blk), P(), P()),
        out_specs=(by_row, P(blk, None), by_row),
        check_vma=False,
    )
```

```python
import jax
import jax.numpy as jnp
from jax import lax
from jax.experimental import pallas as pl
from jax.experimental.pallas import tpu as pltpu
from jax.sharding import Mesh, PartitionSpec as P

epsilon = 1e-06
AXES = ("zh", "x1", "x0", "y", "c", "zl")
f32 = jnp.float32
bf16 = jnp.bfloat16
ROWS = 128
WIDTH = 1152
VMEM = pl.BlockSpec(memory_space=pltpu.VMEM)
SMEM = pl.BlockSpec(memory_space=pltpu.SMEM)
ANY = pl.BlockSpec(memory_space=pl.ANY)
HBM = pl.BlockSpec(memory_space=pltpu.HBM)


def dot(a, b, ca, cb):
    return lax.dot_general(a, b, (((ca,), (cb,)), ((), ())), preferred_element_type=f32)


def xor(x, axis, step):
    size = lax.axis_size(axis)
    return lax.ppermute(x, axis, [(i, i ^ step) for i in range(size)])


def shape(dtype, *dims):
    return jax.ShapeDtypeStruct(dims, dtype)


def in_hbm(x):
    return pltpu.with_memory_space_constraint(x, pltpu.HBM)


def call(body, outs, specs, flops, moved, scratch=(), vmem=8):
    return pl.pallas_call(
        body,
        out_shape=outs,
        in_specs=specs,
        out_specs=[VMEM] * len(outs),
        scratch_shapes=scratch,
        compiler_params=pltpu.CompilerParams(vmem_limit_bytes=vmem << 20),
        cost_estimate=pl.CostEstimate(flops=flops, bytes_accessed=moved, transcendentals=0),
    )


def prepare(count, hidden, text, hid_out, txt_out, hid_in, txt_in, sems):
    copies = [
        pltpu.make_async_copy(text, txt_in, sems.at[0]),
        pltpu.make_async_copy(hidden, hid_in, sems.at[1]),
    ]
    for copy in copies:
        copy.start()
    keep = lax.broadcasted_iota(jnp.int32, (ROWS, 1), 0) < count[0]
    copies[0].wait()
    txt = txt_in[...].astype(f32)
    txt = txt * lax.rsqrt(jnp.sum(txt * txt, axis=1, keepdims=True) + epsilon)
    txt_out[...] = jnp.where(keep, txt, 0.0).astype(bf16)
    copies[1].wait()
    hid_out[...] = jnp.where(keep, hid_in[...].astype(f32), 0.0).astype(bf16)


def join(after, own, paired, t1, t3, both, first, second):
    both[:ROWS] = own[...]
    both[ROWS:] = paired[...]
    first[...] = t3[: ROWS // 2]
    second[...] = t1[ROWS // 2 :]


def ahead(after, scale, bias, pair_ids, weight, held, chosen, left, right, settings, sem):
    copy = pltpu.make_async_copy(weight, held, sem)
    copy.start()
    settings[0:1, :] = jnp.full((1, ROWS), scale[0], f32)
    settings[1:2, :] = jnp.full((1, ROWS), bias[0], f32)
    zh, x1, x0, y, c, zl = (lax.axis_index(a) for a in AXES)
    row = lax.broadcasted_iota(jnp.int32, (576, 1), 0)
    k, row = row // 144, row % 144
    j, row = row // 36, row % 36
    m, r = row // 9, row % 9
    turn = jnp.where(zl == 0, 4 - m, m)
    owner = (zh + turn) % 4
    core = (c + owner + zh) % 2
    place = owner * 288 + (k ^ (x1 * 2 + x0)) * 72 + (j ^ y) * 18 + core * 9 + r
    spots = lax.broadcasted_iota(jnp.int32, (576, WIDTH), 1)
    chosen[...] = (spots == place).astype(f32).astype(bf16)
    base = (zh * 2 + x1) * 16

    def label(px, py, pc):
        start = pl.multiple_of((base + (px * 4 + py) * 2 + pc) * ROWS, ROWS)
        return pair_ids[:, pl.ds(start, ROWS)]

    for k, (px, pc) in enumerate(((x0, c), (1 - x0, c), (x0, 1 - c), (1 - x0, 1 - c))):
        tall = jnp.transpose(jnp.broadcast_to(label(px, y, pc), (8, ROWS)))
        left[k * ROWS : (k + 1) * ROWS, :] = tall[:, :1]
    for j in range(4):
        right[:, j * ROWS : (j + 1) * ROWS] = label(x0, y ^ j, c)
    copy.wait()


def project(both, cores, weight, chosen, embed, normed, inverse, turned):
    hid = jnp.concatenate([both[...], cores[...]], 0)
    projected = dot(hid, weight[...], 1, 0)
    turned[...] = dot(chosen[...], hid, 1, 1).astype(bf16)
    inv = lax.rsqrt(jnp.sum(projected * projected, axis=1, keepdims=True) + epsilon)
    unit = projected * inv
    normed[...] = unit
    embed[...] = unit.astype(bf16)
    inverse[...] = inv


def coefficients(settings, left, right, embed, txt):
    scale, bias = settings[0:1, 0:1], settings[1:2, 0:1]
    scores = scale * dot(embed, txt, 1, 1) + bias
    target = jnp.where(left == right, 1.0, -1.0).astype(f32)
    return (-target * jax.nn.sigmoid(-target * scores) * scale).astype(bf16)


def near_tile(settings, left, right, embed, t0, t1, t3, coef_out, grad):
    txt = jnp.concatenate([t0[...], t1[...], t3[...]], 0)
    there = jnp.concatenate([right[:, : 2 * ROWS], right[:, 3 * ROWS :]], 1)
    coef = coefficients(settings, left[...], there, embed[...], txt)
    coef_out[...] = coef
    grad[...] = dot(coef, txt, 1, 0)


def far_tile(settings, left, right, embed, normed, inverse, t2a, t2b, near, coef_out, part_out, part_send):
    txt = jnp.concatenate([t2a[...], t2b[...]], 0)
    coef = coefficients(settings, left[...], right[:, 2 * ROWS : 3 * ROWS], embed[...], txt)
    coef_out[...] = coef
    grad = near[...] + dot(coef, txt, 1, 0)
    unit = normed[...]
    radial = jnp.sum(unit * grad, axis=1, keepdims=True)
    part = (grad - unit * radial) * inverse[...]
    part_out[...] = part
    part_send[...] = part.astype(bf16)


def text_terms(near, far, embed, terms, t2):
    grad = dot(near[...], embed[...], 0, 0)
    terms[: 2 * ROWS, :] = grad[: 2 * ROWS]
    terms[3 * ROWS :, :] = grad[2 * ROWS :]
    t2[...] = dot(far[...], embed[...], 0, 0).astype(bf16)


def weight_terms(part, arrived, turned, terms, rows, own, s1, s2, s3, t1, t3):
    half = 2 * ROWS
    top = part[:half] + arrived[half:].astype(f32)
    low = part[half:] + arrived[:half].astype(f32)
    rows[...] = top
    grad = dot(turned[...], jnp.concatenate([top, low], 0).astype(bf16), 1, 0)
    own[...] = grad[:144]
    for k, out in enumerate((s1, s2, s3)):
        out[...] = grad[(k + 1) * 144 : (k + 2) * 144].astype(bf16)
    t1[...] = terms[ROWS : 2 * ROWS].astype(bf16)
    t3[...] = terms[3 * ROWS :].astype(bf16)


def first_sum(own, a1, a3, a2, b1, b2, b3, out, s1, s2, s3, held):
    held[...] = own[...] + a2[...].astype(f32) + a1[...].astype(f32) + a3[...].astype(f32)
    out[...] = held[:36]
    for k, send in enumerate((s1, s2, s3)):
        send[...] = held[(k + 1) * 36 : (k + 2) * 36].astype(bf16)


def second_sum(own, a2, a1, a3, rows, keep, send, rows_send, held):
    total = own[...] + a2[...].astype(f32) + a1[...].astype(f32) + a3[...].astype(f32)
    total = total.astype(bf16).astype(f32)
    held[...] = total
    keep[...] = total
    send[...] = jnp.concatenate([held[:9], held[18:]], 0).astype(bf16)
    rows_send[...] = rows[ROWS:].astype(bf16)


def third_sum(own, arrived, out, near, far, held):
    held[...] = arrived[...].astype(f32)
    out[...] = own[:9] + held[:9]
    near[...] = (own[9:18] + held[18:]).astype(bf16)
    far[...] = (own[18:27] + held[9:18]).astype(bf16)


def last_sum(after, own, a1, a3, a2, out):
    sides = a1[...].astype(f32) + a2[...].astype(f32)
    out[...] = own[...] + sides + a3[...].astype(f32)


def text_sum(after, count, terms, b1, b2, b3, out):
    keep = lax.broadcasted_iota(jnp.int32, (ROWS, 1), 0) < count[0]
    total = terms[:ROWS] + b2[...].astype(f32) + b1[...].astype(f32) + b3[...].astype(f32)
    out[...] = jnp.where(keep, total, 0.0)


def back(count, rows, arrived, weight, out, done):
    total = (rows[:ROWS] + arrived[...].astype(f32)).astype(bf16)
    grad = dot(total, weight[...], 1, 1)
    keep = lax.broadcasted_iota(jnp.int32, (ROWS, 1), 0) < count[0]
    out[...] = jnp.where(keep, grad, 0.0).astype(bf16)
    done[...] = jnp.zeros((8, ROWS), f32)


def along_z(x, hop, cross):
    pairs = []
    for z in range(8):
        to = (z + (hop if z % 2 else -hop)) % 8
        for c in range(2):
            pairs.append((z // 2 * 4 + c * 2 + z % 2, to // 2 * 4 + (c ^ cross) * 2 + to % 2))
    return lax.ppermute(x, ("zh", "c", "zl"), pairs)


def per_device(hidden, weight, text, pair_ids, valid_count, logit_scale, logit_bias):
    X = ("x1", "x0")
    block = ROWS * WIDTH
    wide, tall = shape(bf16, ROWS, WIDTH), shape(f32, 512, WIDTH)
    with jax.named_scope("prepare"):
        hid, txt = call(
            prepare,
            [wide, wide],
            [SMEM, HBM, HBM],
            0,
            block,
            [pltpu.VMEM((ROWS, WIDTH), bf16)] * 2 + [pltpu.SemaphoreType.DMA((2,))],
        )(valid_count, in_hbm(hidden), in_hbm(text))
    with jax.named_scope("gather"):
        hid_x = xor(hid, "x0", 1)
        txt_1 = xor(txt, "y", 1)
        txt_3 = xor(txt, "y", 3)
        held, chosen, left, right, settings = call(
            ahead,
            [
                shape(bf16, WIDTH, WIDTH),
                shape(bf16, 576, WIDTH),
                shape(jnp.int32, 512, 1),
                shape(jnp.int32, 1, 512),
                shape(f32, 2, ROWS),
            ],
            [ANY, SMEM, SMEM, VMEM, HBM],
            block * 1000,
            block,
            [pltpu.SemaphoreType.DMA],
        )(hid, logit_scale.reshape(1), logit_bias.reshape(1), pair_ids, in_hbm(weight))
        both, first, second = call(
            join,
            [shape(bf16, 256, WIDTH)] + [shape(bf16, 64, WIDTH)] * 2,
            [ANY] + [VMEM] * 4,
            0,
            block,
        )(chosen, hid, hid_x, txt_1, txt_3)
        hid_c = xor(both, "c", 1)
        txt_2a = xor(first, "y", 1)
        txt_2b = xor(second, "y", 3)
    with jax.named_scope("project"):
        embed, normed, inverse, turned = call(
            project,
            [shape(bf16, 512, WIDTH), tall, shape(f32, 512, 1), shape(bf16, 576, 512)],
            [VMEM] * 4,
            0,
            block,
            vmem=16,
        )(both, hid_c, held, chosen)
    with jax.named_scope("tile"):
        coef, grad = call(
            near_tile, [shape(bf16, 512, 384), tall], [VMEM] * 7, 0, block, vmem=16
        )(settings, left, right, embed, txt, txt_1, txt_3)
        coef_2, part, part_send = call(
            far_tile,
            [shape(bf16, 512, ROWS), tall, shape(bf16, 512, WIDTH)],
            [VMEM] * 9,
            0,
            block,
            vmem=16,
        )(settings, left, right, embed, normed, inverse, txt_2a, txt_2b, grad)
    with jax.named_scope("core"):
        arrived = xor(part_send, "c", 1)
    with jax.named_scope("text"):
        terms, u2 = call(text_terms, [tall, wide], [VMEM] * 3, 0, block)(coef, coef_2, embed)
        u2 = xor(u2, "y", 2)
    with jax.named_scope("weight"):
        rows, own, s1, s2, s3, u1, u3 = call(
            weight_terms,
            [shape(f32, 256, WIDTH), shape(f32, 144, WIDTH)]
            + [shape(bf16, 144, WIDTH)] * 3
            + [wide] * 2,
            [VMEM] * 4,
            0,
            block,
            vmem=16,
        )(part, arrived, turned, terms)
        s2, s1, s3 = xor(s2, X, 2), xor(s1, X, 1), xor(s3, X, 3)
        u1, u3 = xor(u1, "y", 1), xor(u3, "y", 3)
        small, small_b = shape(f32, 36, WIDTH), shape(bf16, 36, WIDTH)
        whole, s1, s2, s3 = call(
            first_sum,
            [small] + [small_b] * 3,
            [VMEM] * 4 + [ANY] * 3,
            0,
            block,
            [pltpu.VMEM((144, WIDTH), f32)],
        )(own, s1, s3, s2, u1, u2, u3)
        s2, s1, s3 = xor(s2, "y", 2), xor(s1, "y", 1), xor(s3, "y", 3)
        whole, whole_send, rows_send = call(
            second_sum,
            [small, shape(bf16, 27, WIDTH), wide],
            [VMEM] * 5,
            0,
            block,
            [pltpu.VMEM((36, WIDTH), f32)],
        )(whole, s2, s1, s3, rows)
        arrived = xor(whole_send, "zl", 1)
        whole, near, far = call(
            third_sum,
            [shape(f32, 9, WIDTH)] + [shape(bf16, 9, WIDTH)] * 2,
            [VMEM] * 2,
            0,
            block,
            [pltpu.VMEM((27, WIDTH), f32)],
        )(whole, arrived)
        got = [along_z(near, 1, 1), along_z(far, 3, 0), along_z(near, 2, 1)]
    with jax.named_scope("hidden"):
        rows_x = xor(rows_send, "x0", 1)
        hidden_grad, done = call(
            back, [wide, shape(f32, 8, ROWS)], [SMEM] + [VMEM] * 3, 2 * block * WIDTH, WIDTH * WIDTH * 2
        )(valid_count, rows, rows_x, held)
    with jax.named_scope("weight"):
        (weight_grad,) = call(last_sum, [shape(f32, 9, WIDTH)], [ANY] + [VMEM] * 4, 0, block)(
            done, whole, *got
        )
    with jax.named_scope("text"):
        (text_grad,) = call(
            text_sum, [shape(f32, ROWS, WIDTH)], [ANY, SMEM] + [VMEM] * 4, 0, block * 16
        )(whole_send, valid_count, terms, u1, u2, u3)
    return hidden_grad, weight_grad, text_grad


def solution(mesh):
    fine = Mesh(mesh.devices.reshape(4, 2, 2, 4, 2, 2), AXES)
    blk = ("zh", "x1", "x0", "y", "c")
    by_row = P(("zl",) + blk, None)
    return jax.shard_map(
        per_device,
        mesh=fine,
        in_specs=(by_row, P(), by_row, P("zl", None), P(("zl",) + blk), P(), P()),
        out_specs=(by_row, P(blk, None), by_row),
        check_vma=False,
    )
```

```python
import jax
import jax.numpy as jnp
from jax import lax
from jax.experimental import pallas as pl
from jax.experimental.pallas import tpu as pltpu
from jax.sharding import Mesh, PartitionSpec as P

epsilon = 1e-06
AXES = ("zh", "x1", "x0", "y", "c", "zl")
f32 = jnp.float32
bf16 = jnp.bfloat16
ROWS = 128
WIDTH = 1152
CUT = 80
VMEM = pl.BlockSpec(memory_space=pltpu.VMEM)
SMEM = pl.BlockSpec(memory_space=pltpu.SMEM)
ANY = pl.BlockSpec(memory_space=pl.ANY)
HBM = pl.BlockSpec(memory_space=pltpu.HBM)


def dot(a, b, ca, cb):
    return lax.dot_general(a, b, (((ca,), (cb,)), ((), ())), preferred_element_type=f32)


def xor(x, axis, step):
    size = lax.axis_size(axis)
    return lax.ppermute(x, axis, [(i, i ^ step) for i in range(size)])


def shape(dtype, *dims):
    return jax.ShapeDtypeStruct(dims, dtype)


def in_hbm(x):
    return pltpu.with_memory_space_constraint(x, pltpu.HBM)


def call(body, outs, specs, flops, moved, scratch=(), vmem=8):
    return pl.pallas_call(
        body,
        out_shape=outs,
        in_specs=specs,
        out_specs=[VMEM] * len(outs),
        scratch_shapes=scratch,
        compiler_params=pltpu.CompilerParams(vmem_limit_bytes=vmem << 20),
        cost_estimate=pl.CostEstimate(flops=flops, bytes_accessed=moved, transcendentals=0),
    )


def prepare(count, hidden, text, hid_out, txt_out, hid_in, txt_in, sems):
    copies = [
        pltpu.make_async_copy(text, txt_in, sems.at[0]),
        pltpu.make_async_copy(hidden, hid_in, sems.at[1]),
    ]
    for copy in copies:
        copy.start()
    keep = lax.broadcasted_iota(jnp.int32, (ROWS, 1), 0) < count[0]
    copies[0].wait()
    txt = txt_in[...].astype(f32)
    txt = txt * lax.rsqrt(jnp.sum(txt * txt, axis=1, keepdims=True) + epsilon)
    txt_out[...] = jnp.where(keep, txt, 0.0).astype(bf16)
    copies[1].wait()
    hid_out[...] = jnp.where(keep, hid_in[...].astype(f32), 0.0).astype(bf16)


def join(after, own, paired, t1, t3, both, first, second):
    both[:ROWS] = own[...]
    both[ROWS:] = paired[...]
    first[...] = t3[:CUT]
    second[...] = t1[CUT:]


def ahead(after, scale, bias, pair_ids, weight, held, chosen, left, right, settings, sem):
    copy = pltpu.make_async_copy(weight, held, sem)
    copy.start()
    settings[0:1, :] = jnp.full((1, ROWS), scale[0], f32)
    settings[1:2, :] = jnp.full((1, ROWS), bias[0], f32)
    zh, x1, x0, y, c, zl = (lax.axis_index(a) for a in AXES)
    row = lax.broadcasted_iota(jnp.int32, (576, 1), 0)
    k, row = row // 144, row % 144
    j, row = row // 36, row % 36
    m, r = row // 9, row % 9
    turn = jnp.where(zl == 0, 4 - m, m)
    owner = (zh + turn) % 4
    core = (c + owner + zh) % 2
    place = owner * 288 + (k ^ (x1 * 2 + x0)) * 72 + (j ^ y) * 18 + core * 9 + r
    spots = lax.broadcasted_iota(jnp.int32, (576, WIDTH), 1)
    chosen[...] = (spots == place).astype(f32).astype(bf16)
    base = (zh * 2 + x1) * 16

    def label(px, py, pc):
        start = pl.multiple_of((base + (px * 4 + py) * 2 + pc) * ROWS, ROWS)
        return pair_ids[:, pl.ds(start, ROWS)]

    for k, (px, pc) in enumerate(((x0, c), (1 - x0, c), (x0, 1 - c), (1 - x0, 1 - c))):
        tall = jnp.transpose(jnp.broadcast_to(label(px, y, pc), (8, ROWS)))
        left[k * ROWS : (k + 1) * ROWS, :] = tall[:, :1]
    for j in range(4):
        right[:, j * ROWS : (j + 1) * ROWS] = label(x0, y ^ j, c)
    copy.wait()


def project(both, cores, weight, chosen, embed, normed, inverse, turned):
    hid = jnp.concatenate([both[...], cores[...]], 0)
    projected = dot(hid, weight[...], 1, 0)
    turned[...] = dot(chosen[...], hid, 1, 1).astype(bf16)
    inv = lax.rsqrt(jnp.sum(projected * projected, axis=1, keepdims=True) + epsilon)
    unit = projected * inv
    normed[...] = unit
    embed[...] = unit.astype(bf16)
    inverse[...] = inv


def coefficients(settings, left, right, embed, txt):
    scale, bias = settings[0:1, 0:1], settings[1:2, 0:1]
    scores = scale * dot(embed, txt, 1, 1) + bias
    target = jnp.where(left == right, 1.0, -1.0).astype(f32)
    return (-target * jax.nn.sigmoid(-target * scores) * scale).astype(bf16)


def near_tile(settings, left, right, embed, t0, t1, t3, coef_out, grad):
    txt = jnp.concatenate([t0[...], t1[...], t3[...]], 0)
    there = jnp.concatenate([right[:, : 2 * ROWS], right[:, 3 * ROWS :]], 1)
    coef = coefficients(settings, left[...], there, embed[...], txt)
    coef_out[...] = coef
    grad[...] = dot(coef, txt, 1, 0)


def far_tile(settings, left, right, embed, normed, inverse, t2a, t2b, near, coef_out, part_out, part_send):
    txt = jnp.concatenate([t2a[...], t2b[...]], 0)
    coef = coefficients(settings, left[...], right[:, 2 * ROWS : 3 * ROWS], embed[...], txt)
    coef_out[...] = coef
    grad = near[...] + dot(coef, txt, 1, 0)
    unit = normed[...]
    radial = jnp.sum(unit * grad, axis=1, keepdims=True)
    part = (grad - unit * radial) * inverse[...]
    part_out[...] = part
    part_send[...] = part.astype(bf16)


def text_terms(near, far, embed, terms, t2):
    grad = dot(near[...], embed[...], 0, 0)
    terms[: 2 * ROWS, :] = grad[: 2 * ROWS]
    terms[3 * ROWS :, :] = grad[2 * ROWS :]
    t2[...] = dot(far[...], embed[...], 0, 0).astype(bf16)


def weight_terms(part, arrived, turned, terms, rows, own, s1, s2, s3, t1, t3):
    half = 2 * ROWS
    top = part[:half] + arrived[half:].astype(f32)
    low = part[half:] + arrived[:half].astype(f32)
    rows[...] = top
    grad = dot(turned[...], jnp.concatenate([top, low], 0).astype(bf16), 1, 0)
    own[...] = grad[:144]
    for k, out in enumerate((s1, s2, s3)):
        out[...] = grad[(k + 1) * 144 : (k + 2) * 144].astype(bf16)
    t1[...] = terms[ROWS : 2 * ROWS].astype(bf16)
    t3[...] = terms[3 * ROWS :].astype(bf16)


def first_sum(own, a1, a3, a2, b1, b2, b3, out, s1, s2, s3, held):
    held[...] = own[...] + a2[...].astype(f32) + a1[...].astype(f32) + a3[...].astype(f32)
    out[...] = held[:36]
    for k, send in enumerate((s1, s2, s3)):
        send[...] = held[(k + 1) * 36 : (k + 2) * 36].astype(bf16)


def second_sum(own, a2, a1, a3, rows, keep, send, rows_send, held):
    total = own[...] + a2[...].astype(f32) + a1[...].astype(f32) + a3[...].astype(f32)
    total = total.astype(bf16).astype(f32)
    held[...] = total
    keep[...] = total
    send[...] = jnp.concatenate([held[:9], held[18:]], 0).astype(bf16)
    rows_send[...] = rows[ROWS:].astype(bf16)


def third_sum(own, arrived, out, near, far, held):
    held[...] = arrived[...].astype(f32)
    out[...] = own[:9] + held[:9]
    near[...] = (own[9:18] + held[18:]).astype(bf16)
    far[...] = (own[18:27] + held[9:18]).astype(bf16)


def last_sum(after, own, a1, a3, a2, out):
    sides = a1[...].astype(f32) + a2[...].astype(f32)
    out[...] = own[...] + sides + a3[...].astype(f32)


def text_sum(after, count, terms, b1, b2, b3, out):
    keep = lax.broadcasted_iota(jnp.int32, (ROWS, 1), 0) < count[0]
    total = terms[:ROWS] + b2[...].astype(f32) + b1[...].astype(f32) + b3[...].astype(f32)
    out[...] = jnp.where(keep, total, 0.0)


def back(count, rows, arrived, weight, out, done):
    total = (rows[:ROWS] + arrived[...].astype(f32)).astype(bf16)
    grad = dot(total, weight[...], 1, 1)
    keep = lax.broadcasted_iota(jnp.int32, (ROWS, 1), 0) < count[0]
    out[...] = jnp.where(keep, grad, 0.0).astype(bf16)
    done[...] = jnp.zeros((8, ROWS), f32)


def along_z(x, hop, cross):
    pairs = []
    for z in range(8):
        to = (z + (hop if z % 2 else -hop)) % 8
        for c in range(2):
            pairs.append((z // 2 * 4 + c * 2 + z % 2, to // 2 * 4 + (c ^ cross) * 2 + to % 2))
    return lax.ppermute(x, ("zh", "c", "zl"), pairs)


def per_device(hidden, weight, text, pair_ids, valid_count, logit_scale, logit_bias):
    X = ("x1", "x0")
    block = ROWS * WIDTH
    wide, tall = shape(bf16, ROWS, WIDTH), shape(f32, 512, WIDTH)
    with jax.named_scope("prepare"):
        hid, txt = call(
            prepare,
            [wide, wide],
            [SMEM, HBM, HBM],
            0,
            block,
            [pltpu.VMEM((ROWS, WIDTH), bf16)] * 2 + [pltpu.SemaphoreType.DMA((2,))],
        )(valid_count, in_hbm(hidden), in_hbm(text))
    with jax.named_scope("gather"):
        hid_x = xor(hid, "x0", 1)
        txt_1 = xor(txt, "y", 1)
        txt_3 = xor(txt, "y", 3)
        held, chosen, left, right, settings = call(
            ahead,
            [
                shape(bf16, WIDTH, WIDTH),
                shape(bf16, 576, WIDTH),
                shape(jnp.int32, 512, 1),
                shape(jnp.int32, 1, 512),
                shape(f32, 2, ROWS),
            ],
            [ANY, SMEM, SMEM, VMEM, HBM],
            block * 1000,
            block,
            [pltpu.SemaphoreType.DMA],
        )(hid, logit_scale.reshape(1), logit_bias.reshape(1), pair_ids, in_hbm(weight))
        both, first, second = call(
            join,
            [shape(bf16, 256, WIDTH), shape(bf16, CUT, WIDTH), shape(bf16, ROWS - CUT, WIDTH)],
            [ANY] + [VMEM] * 4,
            0,
            block,
        )(chosen, hid, hid_x, txt_1, txt_3)
        hid_c = xor(both, "c", 1)
        txt_2a = xor(first, "y", 1)
        txt_2b = xor(second, "y", 3)
    with jax.named_scope("project"):
        embed, normed, inverse, turned = call(
            project,
            [shape(bf16, 512, WIDTH), tall, shape(f32, 512, 1), shape(bf16, 576, 512)],
            [VMEM] * 4,
            0,
            block,
            vmem=16,
        )(both, hid_c, held, chosen)
    with jax.named_scope("tile"):
        coef, grad = call(
            near_tile, [shape(bf16, 512, 384), tall], [VMEM] * 7, 0, block, vmem=16
        )(settings, left, right, embed, txt, txt_1, txt_3)
        coef_2, part, part_send = call(
            far_tile,
            [shape(bf16, 512, ROWS), tall, shape(bf16, 512, WIDTH)],
            [VMEM] * 9,
            0,
            block,
            vmem=16,
        )(settings, left, right, embed, normed, inverse, txt_2a, txt_2b, grad)
    with jax.named_scope("core"):
        arrived = xor(part_send, "c", 1)
    with jax.named_scope("text"):
        terms, u2 = call(text_terms, [tall, wide], [VMEM] * 3, 0, block)(coef, coef_2, embed)
        u2 = xor(u2, "y", 2)
    with jax.named_scope("weight"):
        rows, own, s1, s2, s3, u1, u3 = call(
            weight_terms,
            [shape(f32, 256, WIDTH), shape(f32, 144, WIDTH)]
            + [shape(bf16, 144, WIDTH)] * 3
            + [wide] * 2,
            [VMEM] * 4,
            0,
            block,
            vmem=16,
        )(part, arrived, turned, terms)
        s2, s1, s3 = xor(s2, X, 2), xor(s1, X, 1), xor(s3, X, 3)
        u1, u3 = xor(u1, "y", 1), xor(u3, "y", 3)
        small, small_b = shape(f32, 36, WIDTH), shape(bf16, 36, WIDTH)
        whole, s1, s2, s3 = call(
            first_sum,
            [small] + [small_b] * 3,
            [VMEM] * 4 + [ANY] * 3,
            0,
            block,
            [pltpu.VMEM((144, WIDTH), f32)],
        )(own, s1, s3, s2, u1, u2, u3)
        s2, s1, s3 = xor(s2, "y", 2), xor(s1, "y", 1), xor(s3, "y", 3)
        whole, whole_send, rows_send = call(
            second_sum,
            [small, shape(bf16, 27, WIDTH), wide],
            [VMEM] * 5,
            0,
            block,
            [pltpu.VMEM((36, WIDTH), f32)],
        )(whole, s2, s1, s3, rows)
        arrived = xor(whole_send, "zl", 1)
        whole, near, far = call(
            third_sum,
            [shape(f32, 9, WIDTH)] + [shape(bf16, 9, WIDTH)] * 2,
            [VMEM] * 2,
            0,
            block,
            [pltpu.VMEM((27, WIDTH), f32)],
        )(whole, arrived)
        got = [along_z(near, 1, 1), along_z(far, 3, 0), along_z(near, 2, 1)]
    with jax.named_scope("hidden"):
        rows_x = xor(rows_send, "x0", 1)
        hidden_grad, done = call(
            back, [wide, shape(f32, 8, ROWS)], [SMEM] + [VMEM] * 3, 2 * block * WIDTH, WIDTH * WIDTH * 2
        )(valid_count, rows, rows_x, held)
    with jax.named_scope("weight"):
        (weight_grad,) = call(last_sum, [shape(f32, 9, WIDTH)], [ANY] + [VMEM] * 4, 0, block)(
            done, whole, *got
        )
    with jax.named_scope("text"):
        (text_grad,) = call(
            text_sum, [shape(f32, ROWS, WIDTH)], [ANY, SMEM] + [VMEM] * 4, 0, block * 16
        )(whole_send, valid_count, terms, u1, u2, u3)
    return hidden_grad, weight_grad, text_grad


def solution(mesh):
    fine = Mesh(mesh.devices.reshape(4, 2, 2, 4, 2, 2), AXES)
    blk = ("zh", "x1", "x0", "y", "c")
    by_row = P(("zl",) + blk, None)
    return jax.shard_map(
        per_device,
        mesh=fine,
        in_specs=(by_row, P(), by_row, P("zl", None), P(("zl",) + blk), P(), P()),
        out_specs=(by_row, P(blk, None), by_row),
        check_vma=False,
    )
```

```python
import jax
import jax.numpy as jnp
from jax import lax
from jax.experimental import pallas as pl
from jax.experimental.pallas import tpu as pltpu
from jax.sharding import Mesh, PartitionSpec as P

epsilon = 1e-06
AXES = ("zh", "x1", "x0", "y", "c", "zl")
f32 = jnp.float32
bf16 = jnp.bfloat16
ROWS = 128
WIDTH = 1152
CUT = 80
VMEM = pl.BlockSpec(memory_space=pltpu.VMEM)
SMEM = pl.BlockSpec(memory_space=pltpu.SMEM)
ANY = pl.BlockSpec(memory_space=pl.ANY)
HBM = pl.BlockSpec(memory_space=pltpu.HBM)


def dot(a, b, ca, cb):
    return lax.dot_general(a, b, (((ca,), (cb,)), ((), ())), preferred_element_type=f32)


def xor(x, axis, step):
    size = lax.axis_size(axis)
    return lax.ppermute(x, axis, [(i, i ^ step) for i in range(size)])


def shape(dtype, *dims):
    return jax.ShapeDtypeStruct(dims, dtype)


def in_hbm(x):
    return pltpu.with_memory_space_constraint(x, pltpu.HBM)


def call(body, outs, specs, flops, moved, scratch=(), vmem=8):
    return pl.pallas_call(
        body,
        out_shape=outs,
        in_specs=specs,
        out_specs=[VMEM] * len(outs),
        scratch_shapes=scratch,
        compiler_params=pltpu.CompilerParams(vmem_limit_bytes=vmem << 20),
        cost_estimate=pl.CostEstimate(flops=flops, bytes_accessed=moved, transcendentals=0),
    )


def prepare(count, hidden, text, hid_out, txt_out, hid_in, txt_in, sems):
    copies = [
        pltpu.make_async_copy(text, txt_in, sems.at[0]),
        pltpu.make_async_copy(hidden, hid_in, sems.at[1]),
    ]
    for copy in copies:
        copy.start()
    keep = lax.broadcasted_iota(jnp.int32, (ROWS, 1), 0) < count[0]
    copies[0].wait()
    txt = txt_in[...].astype(f32)
    txt = txt * lax.rsqrt(jnp.sum(txt * txt, axis=1, keepdims=True) + epsilon)
    txt_out[...] = jnp.where(keep, txt, 0.0).astype(bf16)
    copies[1].wait()
    hid_out[...] = jnp.where(keep, hid_in[...].astype(f32), 0.0).astype(bf16)


def join(after, own, paired, t1, t3, both, first, second):
    both[:ROWS] = own[...]
    both[ROWS:] = paired[...]
    first[...] = t3[:CUT]
    second[...] = t1[CUT:]


def ahead(after, scale, bias, pair_ids, weight, held, chosen, left, right, settings, sem):
    copy = pltpu.make_async_copy(weight, held, sem)
    copy.start()
    settings[0:1, :] = jnp.full((1, ROWS), scale[0], f32)
    settings[1:2, :] = jnp.full((1, ROWS), bias[0], f32)
    zh, x1, x0, y, c, zl = (lax.axis_index(a) for a in AXES)
    row = lax.broadcasted_iota(jnp.int32, (576, 1), 0)
    k, row = row // 144, row % 144
    j, row = row // 36, row % 36
    m, r = row // 9, row % 9
    turn = jnp.where(zl == 0, 4 - m, m)
    owner = (zh + turn) % 4
    core = (c + owner + zh) % 2
    place = owner * 288 + (k ^ (x1 * 2 + x0)) * 72 + (j ^ y) * 18 + core * 9 + r
    spots = lax.broadcasted_iota(jnp.int32, (576, WIDTH), 1)
    chosen[...] = (spots == place).astype(f32).astype(bf16)
    base = (zh * 2 + x1) * 16

    def label(px, py, pc):
        start = pl.multiple_of((base + (px * 4 + py) * 2 + pc) * ROWS, ROWS)
        return pair_ids[:, pl.ds(start, ROWS)]

    for k, (px, pc) in enumerate(((x0, c), (1 - x0, c), (x0, 1 - c), (1 - x0, 1 - c))):
        tall = jnp.transpose(jnp.broadcast_to(label(px, y, pc), (8, ROWS)))
        left[k * ROWS : (k + 1) * ROWS, :] = tall[:, :1]
    for j in range(4):
        right[:, j * ROWS : (j + 1) * ROWS] = label(x0, y ^ j, c)
    copy.wait()


def project(both, cores, weight, chosen, embed, normed, inverse, turned):
    hid = jnp.concatenate([both[...], cores[...]], 0)
    projected = dot(hid, weight[...], 1, 0)
    turned[...] = dot(chosen[...], hid, 1, 1).astype(bf16)
    inv = lax.rsqrt(jnp.sum(projected * projected, axis=1, keepdims=True) + epsilon)
    unit = projected * inv
    normed[...] = unit
    embed[...] = unit.astype(bf16)
    inverse[...] = inv


def coefficients(settings, left, right, embed, txt):
    scale, bias = settings[0:1, 0:1], settings[1:2, 0:1]
    scores = scale * dot(embed, txt, 1, 1) + bias
    target = jnp.where(left == right, 1.0, -1.0).astype(f32)
    return (-target * jax.nn.sigmoid(-target * scores) * scale).astype(bf16)


def near_tile(settings, left, right, embed, t0, t1, t3, coef_out, grad):
    txt = jnp.concatenate([t0[...], t1[...], t3[...]], 0)
    there = jnp.concatenate([right[:, : 2 * ROWS], right[:, 3 * ROWS :]], 1)
    coef = coefficients(settings, left[...], there, embed[...], txt)
    coef_out[...] = coef
    grad[...] = dot(coef, txt, 1, 0)


def far_tile(settings, left, right, embed, normed, inverse, t2a, t2b, near, coef_out, part_out, part_send):
    txt = jnp.concatenate([t2a[...], t2b[...]], 0)
    coef = coefficients(settings, left[...], right[:, 2 * ROWS : 3 * ROWS], embed[...], txt)
    coef_out[...] = coef
    grad = near[...] + dot(coef, txt, 1, 0)
    unit = normed[...]
    radial = jnp.sum(unit * grad, axis=1, keepdims=True)
    part = (grad - unit * radial) * inverse[...]
    part_out[...] = part
    part_send[...] = part.astype(bf16)


def far_text(far, embed, t2):
    t2[...] = dot(far[...], embed[...], 0, 0).astype(bf16)


def near_text(after, near, embed, own, t1, t3):
    grad = dot(near[...], embed[...], 0, 0)
    own[...] = grad[:ROWS]
    t1[...] = grad[ROWS : 2 * ROWS].astype(bf16)
    t3[...] = grad[2 * ROWS :].astype(bf16)


def weight_terms(part, arrived, turned, rows, own, s1, s2, s3):
    half = 2 * ROWS
    top = part[:half] + arrived[half:].astype(f32)
    low = part[half:] + arrived[:half].astype(f32)
    rows[...] = top
    grad = dot(turned[...], jnp.concatenate([top, low], 0).astype(bf16), 1, 0)
    own[...] = grad[:144]
    for k, out in enumerate((s1, s2, s3)):
        out[...] = grad[(k + 1) * 144 : (k + 2) * 144].astype(bf16)


def first_sum(own, a1, a3, a2, b1, b2, b3, out, s1, s2, s3, held):
    held[...] = own[...] + a2[...].astype(f32) + a1[...].astype(f32) + a3[...].astype(f32)
    out[...] = held[:36]
    for k, send in enumerate((s1, s2, s3)):
        send[...] = held[(k + 1) * 36 : (k + 2) * 36].astype(bf16)


def second_sum(own, a2, a1, a3, rows, keep, send, rows_send, held):
    total = own[...] + a2[...].astype(f32) + a1[...].astype(f32) + a3[...].astype(f32)
    total = total.astype(bf16).astype(f32)
    held[...] = total
    keep[...] = total
    send[...] = jnp.concatenate([held[:9], held[18:]], 0).astype(bf16)
    rows_send[...] = rows[ROWS:].astype(bf16)


def third_sum(own, arrived, out, near, far, held):
    held[...] = arrived[...].astype(f32)
    out[...] = own[:9] + held[:9]
    near[...] = (own[9:18] + held[18:]).astype(bf16)
    far[...] = (own[18:27] + held[9:18]).astype(bf16)


def last_sum(after, own, a1, a3, a2, out):
    sides = a1[...].astype(f32) + a2[...].astype(f32)
    out[...] = own[...] + sides + a3[...].astype(f32)


def text_sum(after, count, terms, b1, b2, b3, out):
    keep = lax.broadcasted_iota(jnp.int32, (ROWS, 1), 0) < count[0]
    total = terms[...] + b2[...].astype(f32) + b1[...].astype(f32) + b3[...].astype(f32)
    out[...] = jnp.where(keep, total, 0.0)


def back(count, rows, arrived, weight, out, done):
    total = (rows[:ROWS] + arrived[...].astype(f32)).astype(bf16)
    grad = dot(total, weight[...], 1, 1)
    keep = lax.broadcasted_iota(jnp.int32, (ROWS, 1), 0) < count[0]
    out[...] = jnp.where(keep, grad, 0.0).astype(bf16)
    done[...] = jnp.zeros((8, ROWS), f32)


def along_z(x, hop, cross):
    pairs = []
    for z in range(8):
        to = (z + (hop if z % 2 else -hop)) % 8
        for c in range(2):
            pairs.append((z // 2 * 4 + c * 2 + z % 2, to // 2 * 4 + (c ^ cross) * 2 + to % 2))
    return lax.ppermute(x, ("zh", "c", "zl"), pairs)


def per_device(hidden, weight, text, pair_ids, valid_count, logit_scale, logit_bias):
    X = ("x1", "x0")
    block = ROWS * WIDTH
    wide, tall = shape(bf16, ROWS, WIDTH), shape(f32, 512, WIDTH)
    with jax.named_scope("prepare"):
        hid, txt = call(
            prepare,
            [wide, wide],
            [SMEM, HBM, HBM],
            0,
            block,
            [pltpu.VMEM((ROWS, WIDTH), bf16)] * 2 + [pltpu.SemaphoreType.DMA((2,))],
        )(valid_count, in_hbm(hidden), in_hbm(text))
    with jax.named_scope("gather"):
        hid_x = xor(hid, "x0", 1)
        txt_1 = xor(txt, "y", 1)
        txt_3 = xor(txt, "y", 3)
        held, chosen, left, right, settings = call(
            ahead,
            [
                shape(bf16, WIDTH, WIDTH),
                shape(bf16, 576, WIDTH),
                shape(jnp.int32, 512, 1),
                shape(jnp.int32, 1, 512),
                shape(f32, 2, ROWS),
            ],
            [ANY, SMEM, SMEM, VMEM, HBM],
            block * 1000,
            block,
            [pltpu.SemaphoreType.DMA],
        )(hid, logit_scale.reshape(1), logit_bias.reshape(1), pair_ids, in_hbm(weight))
        both, first, second = call(
            join,
            [shape(bf16, 256, WIDTH), shape(bf16, CUT, WIDTH), shape(bf16, ROWS - CUT, WIDTH)],
            [ANY] + [VMEM] * 4,
            0,
            block,
        )(chosen, hid, hid_x, txt_1, txt_3)
        hid_c = xor(both, "c", 1)
        txt_2a = xor(first, "y", 1)
        txt_2b = xor(second, "y", 3)
    with jax.named_scope("project"):
        embed, normed, inverse, turned = call(
            project,
            [shape(bf16, 512, WIDTH), tall, shape(f32, 512, 1), shape(bf16, 576, 512)],
            [VMEM] * 4,
            0,
            block,
            vmem=16,
        )(both, hid_c, held, chosen)
    with jax.named_scope("tile"):
        coef, grad = call(
            near_tile, [shape(bf16, 512, 384), tall], [VMEM] * 7, 0, block, vmem=16
        )(settings, left, right, embed, txt, txt_1, txt_3)
        coef_2, part, part_send = call(
            far_tile,
            [shape(bf16, 512, ROWS), tall, shape(bf16, 512, WIDTH)],
            [VMEM] * 9,
            0,
            block,
            vmem=16,
        )(settings, left, right, embed, normed, inverse, txt_2a, txt_2b, grad)
    with jax.named_scope("core"):
        arrived = xor(part_send, "c", 1)
    with jax.named_scope("text"):
        (u2,) = call(far_text, [wide], [VMEM] * 2, 0, block)(coef_2, embed)
        u2 = xor(u2, "y", 2)
    with jax.named_scope("weight"):
        rows, own, s1, s2, s3 = call(
            weight_terms,
            [shape(f32, 256, WIDTH), shape(f32, 144, WIDTH)]
            + [shape(bf16, 144, WIDTH)] * 3,
            [VMEM] * 3,
            0,
            block,
            vmem=16,
        )(part, arrived, turned)
        s2, s1, s3 = xor(s2, X, 2), xor(s1, X, 1), xor(s3, X, 3)
        terms, u1, u3 = call(
            near_text, [shape(f32, ROWS, WIDTH), wide, wide], [ANY] + [VMEM] * 2, 0, block
        )(own, coef, embed)
        u1, u3 = xor(u1, "y", 1), xor(u3, "y", 3)
        small, small_b = shape(f32, 36, WIDTH), shape(bf16, 36, WIDTH)
        whole, s1, s2, s3 = call(
            first_sum,
            [small] + [small_b] * 3,
            [VMEM] * 4 + [ANY] * 3,
            0,
            block,
            [pltpu.VMEM((144, WIDTH), f32)],
        )(own, s1, s3, s2, u1, u2, u3)
        s2, s1, s3 = xor(s2, "y", 2), xor(s1, "y", 1), xor(s3, "y", 3)
        whole, whole_send, rows_send = call(
            second_sum,
            [small, shape(bf16, 27, WIDTH), wide],
            [VMEM] * 5,
            0,
            block,
            [pltpu.VMEM((36, WIDTH), f32)],
        )(whole, s2, s1, s3, rows)
        arrived = xor(whole_send, "zl", 1)
        whole, near, far = call(
            third_sum,
            [shape(f32, 9, WIDTH)] + [shape(bf16, 9, WIDTH)] * 2,
            [VMEM] * 2,
            0,
            block,
            [pltpu.VMEM((27, WIDTH), f32)],
        )(whole, arrived)
        got = [along_z(near, 1, 1), along_z(far, 3, 0), along_z(near, 2, 1)]
    with jax.named_scope("hidden"):
        rows_x = xor(rows_send, "x0", 1)
        hidden_grad, done = call(
            back, [wide, shape(f32, 8, ROWS)], [SMEM] + [VMEM] * 3, 2 * block * WIDTH, WIDTH * WIDTH * 2
        )(valid_count, rows, rows_x, held)
    with jax.named_scope("weight"):
        (weight_grad,) = call(last_sum, [shape(f32, 9, WIDTH)], [ANY] + [VMEM] * 4, 0, block)(
            done, whole, *got
        )
    with jax.named_scope("text"):
        (text_grad,) = call(
            text_sum, [shape(f32, ROWS, WIDTH)], [ANY, SMEM] + [VMEM] * 4, 0, block * 16
        )(whole_send, valid_count, terms, u1, u2, u3)
    return hidden_grad, weight_grad, text_grad


def solution(mesh):
    fine = Mesh(mesh.devices.reshape(4, 2, 2, 4, 2, 2), AXES)
    blk = ("zh", "x1", "x0", "y", "c")
    by_row = P(("zl",) + blk, None)
    return jax.shard_map(
        per_device,
        mesh=fine,
        in_specs=(by_row, P(), by_row, P("zl", None), P(("zl",) + blk), P(), P()),
        out_specs=(by_row, P(blk, None), by_row),
        check_vma=False,
    )
```
